128 devices in a mesh: dp: 16 (over z, y), cent: 8 (over x, core).
Axes of the slice: x: 4, y: 4, z: 4, core: 2. Of those that a mesh axis runs over, the one named last changes fastest.
Arguments:
- embeddings: bfloat16 [65536, 768], P('dp'), may hold values from -32 to 32
- centroids: bfloat16 [4096, 768], P('cent', 'dp'), may hold values from -4 to 4
Outputs:
- new_centroids: float32 [4096, 768], P('cent', 'dp')
The draws below stay inside these ranges and needn't reach their ends.
All inputs are finite; a program needn't handle non-finite values.
Results may differ from the reference program's by a relative error of at most 0.002.
Values may be sent and summed in bfloat16 or wider, within the bound.
A program may use at most 64 MiB of HBM per device.

```python
import math
import jax
import jax.numpy as jnp
from jax import lax

D = 768
K = 4096
ITERS = 2
TOKENS = 65536


def shared_parts(key):
    key_dir, key_spread, key_pick = jax.random.split(key, 3)
    direction = jnp.clip(jax.random.normal(key_dir, (K, D), jnp.float32), -3.0, 3.0)
    spread = jax.random.uniform(key_spread, (K, 1), jnp.float32, 0.6, 2.0)
    picks = jax.random.randint(key_pick, (TOKENS,), 0, K)
    return (direction, spread, picks)


def draw_centroids(key, part):
    direction, spread, picks = shared_parts(key)
    position = (jnp.arange(K, dtype=jnp.float32) / K)[:, None]
    values = direction * (0.1 * jnp.power(3.0, position) * spread)
    return jnp.clip(values, -4.0, 4.0).astype(jnp.bfloat16)


def draw_embeddings(key, part):
    direction, spread, picks = shared_parts(key)
    key = jax.random.fold_in(key, 2)
    key_noise, key_scale = jax.random.split(key, 2)
    position = (jnp.arange(TOKENS, dtype=jnp.float32) / TOKENS)[:, None]
    lift = direction[picks] * (2.0 / math.sqrt(D))
    noise = jnp.clip(jax.random.normal(key_noise, (TOKENS, D), jnp.float32), -3.5, 3.5)
    scale = 0.6 * jnp.power(3.0, position) * jax.random.uniform(key_scale, (TOKENS, 1), jnp.float32, 0.6, 2.0)
    values = scale * (noise + lift)
    return jnp.clip(values, -32.0, 32.0).astype(jnp.bfloat16)


def setup_inputs(seed: int = 0) -> dict:
    seeds = jax.random.split(jax.random.key(seed), 3)
    embeddings = draw_embeddings(jax.random.fold_in(seeds[2], 71), 0)
    centroids = draw_centroids(jax.random.fold_in(seeds[2], 71), 0)
    return {"embeddings": embeddings, "centroids": centroids}


def logits_of(piece, centroids):
    return lax.dot_general(piece, centroids, (((1,), (1,)), ((), ())), preferred_element_type=jnp.float32) * (4.0 / math.sqrt(D))

def reference(embeddings, centroids):
    total = embeddings.shape[0]
    step_rows = math.gcd(total, 4096)
    pieces = embeddings.reshape(total // step_rows, step_rows, D)

    def row_pass(col_pot):

        def one(piece):
            z = logits_of(piece, centroids) + col_pot[None, :]
            top = lax.optimization_barrier(jnp.max(z, axis=1))
            return -(top + jnp.log(lax.optimization_barrier(jnp.sum(jnp.exp(z - top[:, None]), axis=1))))
        return lax.map(one, pieces)

    def col_pass(row_pot):

        def one(carry, item):
            piece, pots = item
            z = logits_of(piece, centroids) + pots[:, None]
            peak, acc = carry
            new_peak = jnp.maximum(peak, lax.optimization_barrier(jnp.max(z, axis=0)))
            acc = acc * jnp.exp(peak - new_peak) + lax.optimization_barrier(jnp.sum(jnp.exp(z - new_peak[None, :]), axis=0))
            return ((new_peak, acc), None)
        init = (jnp.full((K,), -1e+30, jnp.float32), jnp.zeros((K,), jnp.float32))
        (peak, acc), _ = lax.scan(one, init, (pieces, row_pot))
        return jnp.log(jnp.float32(total) / K) - (peak + jnp.log(acc))
    col_pot = jnp.zeros((K,), jnp.float32)
    for step in range(ITERS):
        row_pot = row_pass(col_pot)
        col_pot = col_pass(row_pot)
    row_pot = row_pass(col_pot)

    def final(carry, item):
        piece, pots = item
        plan = jnp.exp(logits_of(piece, centroids) + pots[:, None] + col_pot[None, :])
        sums, mass = carry
        mass = mass + lax.optimization_barrier(jnp.sum(plan, axis=0))
        sums = sums + lax.dot_general(plan.astype(jnp.bfloat16), piece, (((0,), (0,)), ((), ())), preferred_element_type=jnp.float32)
        return ((sums, mass), None)
    init = (jnp.zeros((K, D), jnp.float32), jnp.zeros((K,), jnp.float32))
    (sums, mass), _ = lax.scan(final, init, (pieces, row_pot))
    return sums / mass[:, None]
```

```python
import functools
import math

import jax
import jax.numpy as jnp
from jax import lax
from jax.experimental import pallas as pl
from jax.experimental.pallas import tpu as pltpu
from jax.sharding import PartitionSpec as P

MESH = pl.DeviceIdType.MESH
f32 = jnp.float32
bf16 = jnp.bfloat16
LANES = 128
GROUP = 128
ROUNDS = 3
E_PARTS = 4
HALVES = 2


def nt_dot(a, b):
    return lax.dot_general(a, b, (((1,), (1,)), ((), ())), preferred_element_type=f32)


def nn_dot(a, b):
    return lax.dot_general(a, b, (((1,), (0,)), ((), ())), preferred_element_type=f32)


def lse2(parts):
    top = functools.reduce(jnp.maximum, parts)
    return top + jnp.log2(functools.reduce(jnp.add, [jnp.exp2(p - top) for p in parts]))


def to_lanes(col):
    return jnp.broadcast_to(col, (GROUP, LANES)).T[0:1, :]


def to_rows(row):
    return jnp.broadcast_to(row, (LANES, GROUP)).T


def kernel(
    ndp, ncent, chunks,
    e_hbm, c_ref, out_ref,
    e, ct_own, ct, c, b, plan, sums, low,
    row_own, row_in, acc8, pot,
    col_own, col_in, mass_own, mass_in,
    peak, fac, rs_in,
    e_sem, ct_send, ct_recv, row_send, row_recv, col_send, col_recv, mass_send, mass_recv, rs_send, rs_recv,
):
    n, width = e.shape
    k = c.shape[0]
    own = width // ndp
    ny = math.isqrt(ndp)
    nz = ndp // ny
    w = n // (8 * chunks)
    groups = k // GROUP
    half = k // HALVES
    total_ratio = math.log2((n * ndp) / (k * ncent))

    me = lax.axis_index("dp")
    mec = lax.axis_index("cent")
    my_z, my_y = me // ny, me % ny

    offsets = [(dz, dy) for dz in range(nz) for dy in range(ny)][1:]

    def dp_peer(dz, dy):
        return ((my_z + dz) % nz) * ny + (my_y + dy) % ny

    def cent_peer(o):
        return (mec + o) % ncent

    e_copies = []
    step = n // E_PARTS
    for i in range(E_PARTS):
        rows = pl.ds(i * step, step)
        e_copies.append(pltpu.make_async_copy(e_hbm.at[rows], e.at[rows], e_sem.at[i]))
        e_copies[-1].start()

    barrier = pltpu.get_barrier_semaphore()
    for dz, dy in offsets:
        pl.semaphore_signal(barrier, inc=1, device_id={"dp": dp_peer(dz, dy)}, device_id_type=MESH)
    for o in range(1, ncent):
        pl.semaphore_signal(barrier, inc=1, device_id={"cent": cent_peer(o)}, device_id_type=MESH)

    eye = (
        lax.broadcasted_iota(jnp.int32, (own, own), 0) == lax.broadcasted_iota(jnp.int32, (own, own), 1)
    ).astype(f32).astype(bf16)
    ct_own[...] = nt_dot(eye, c_ref[...]).astype(bf16)
    mine = pl.ds(pl.multiple_of(me * own, own), own)
    ct[mine, :] = ct_own[...]

    pl.semaphore_wait(barrier, len(offsets) + ncent - 1)

    for h in range(HALVES):
        cols = pl.ds(h * half, half)
        for dz, dy in offsets:
            pltpu.make_async_remote_copy(
                src_ref=ct_own.at[:, cols], dst_ref=ct.at[mine, cols],
                send_sem=ct_send.at[h], recv_sem=ct_recv.at[h],
                device_id={"dp": dp_peer(dz, dy)}, device_id_type=MESH,
            ).start()

    def wait_ct(sem, h):
        part = ct.at[pl.ds(0, own * (ndp - 1)), pl.ds(h * half, half)]
        pltpu.make_async_copy(part, part, sem.at[h]).wait()

    unit = 4.0 / math.sqrt(width) / math.log(2.0)
    wide = 2 * w

    def send_rows(r, ch):
        for o in range(1, ncent):
            pltpu.make_async_remote_copy(
                src_ref=row_own.at[r, ch], dst_ref=row_in.at[r, ch, o - 1],
                send_sem=row_send.at[r, ch], recv_sem=row_recv.at[r, ch],
                device_id={"cent": cent_peer(o)}, device_id_type=MESH,
            ).start()

    def wait_rows(sem, r, ch):
        part = row_in.at[r, ch]
        pltpu.make_async_copy(part, part, sem.at[r, ch]).wait()

    for h in range(HALVES):
        wait_ct(ct_recv, h)
        rows = pl.ds(h * half, half)
        c[rows, :] = ct[:, rows].T
        for ch in range(chunks):
            for i in range(0, 8, 2):
                at = (ch * 8 + i) * w
                toks = pl.ds(at, wide)
                if h == 0 and at % step == 0:
                    e_copies[at // step].wait()
                x = nt_dot(c[rows, :], e[toks, :]) * unit
                b[rows, toks] = x
                top = jnp.max(x, axis=0, keepdims=True)
                tot = jnp.sum(jnp.exp2(x - top), axis=0, keepdims=True)
                lse = top + jnp.log2(tot)
                if h == 0:
                    acc8[0:1, toks] = lse
                else:
                    lse = lse2([lse, acc8[0:1, toks]])
                    row_own[0, ch, i : i + 1, :] = lse[:, :w]
                    row_own[0, ch, i + 1 : i + 2, :] = lse[:, w:]
            if h == HALVES - 1:
                send_rows(0, ch)

    tiles = n // LANES
    per = w // LANES
    for ch in range(chunks):
        wait_rows(row_recv, 0, ch)
        dense = -lse2([row_own[0, ch]] + [row_in[0, ch, j] for j in range(ncent - 1)])
        for i in range(8):
            pot[0:1, pl.ds((ch * 8 + i) * w, w)] = dense[i : i + 1, :]

    def tile(i):
        return pl.ds(pl.multiple_of(i * LANES, LANES), LANES)

    def send_cols(r):
        for o, (dz, dy) in enumerate(offsets):
            pltpu.make_async_remote_copy(
                src_ref=col_own.at[r], dst_ref=col_in.at[r, o],
                send_sem=col_send.at[r], recv_sem=col_recv.at[r],
                device_id={"dp": dp_peer(dz, dy)}, device_id_type=MESH,
            ).start()

    def wait_cols(sem, r):
        part = col_in.at[r]
        pltpu.make_async_copy(part, part, sem.at[r]).wait()

    for g in range(groups):
        gs = pl.ds(g * GROUP, GROUP)

        def top_step(i, m):
            return jnp.maximum(m, b[gs, tile(i)] + pot[0:1, tile(i)])

        m = lax.fori_loop(0, tiles, top_step, jnp.full((GROUP, LANES), -jnp.inf, f32), unroll=4)
        m = jnp.broadcast_to(jnp.max(m, axis=1, keepdims=True), (GROUP, LANES))
        peak[gs, :] = m

        def exp_step(i, a):
            x = jnp.exp2((b[gs, tile(i)] + pot[0:1, tile(i)]) - m)
            b[gs, tile(i)] = x
            return a + x

        a = lax.fori_loop(0, tiles, exp_step, jnp.zeros((GROUP, LANES), f32), unroll=4)
        lse = m[:, 0:1] + jnp.log2(jnp.sum(a, axis=1, keepdims=True))
        col_own[0, g : g + 1, :] = to_lanes(lse)
    send_cols(0)
    wait_cols(col_recv, 0)
    lse = lse2([col_own[0]] + [col_in[0, j] for j in range(ndp - 1)])
    for g in range(groups):
        gs = pl.ds(g * GROUP, GROUP)
        fac[gs, :] = jnp.exp2((peak[gs, :] - to_rows(lse[g : g + 1, :])) + total_ratio)

    def row_pass(r):
        for g in range(groups):
            gs = pl.ds(g * GROUP, GROUP)
            f = fac[gs, :]

            def step_(i, _):
                x = jnp.sum((b[gs, tile(i)] * f).reshape(GROUP // 8, 8, LANES), axis=0)
                if g > 0:
                    x = x + acc8[:, tile(i)]
                acc8[:, tile(i)] = x
                return 0

            lax.fori_loop(0, tiles, step_, 0, unroll=4)
        for ch in range(chunks):
            for i in range(8):
                s = jnp.sum(acc8[:, pl.ds((ch * 8 + i) * w, w)], axis=0, keepdims=True)
                row_own[r, ch, i : i + 1, :] = s
            send_rows(r, ch)
        for ch in range(chunks):
            wait_rows(row_recv, r, ch)
            dense = row_own[r, ch]
            for j in range(ncent - 1):
                dense = dense + row_in[r, ch, j]
            dense = 1.0 / dense
            for i in range(8):
                pot[0:1, pl.ds((ch * 8 + i) * w, w)] = dense[i : i + 1, :]

    row_pass(1)

    for g in range(groups):
        gs = pl.ds(g * GROUP, GROUP)

        def col_step(i, a):
            return a + b[gs, tile(i)] * pot[0:1, tile(i)]

        a = lax.fori_loop(0, tiles, col_step, jnp.zeros((GROUP, LANES), f32), unroll=4)
        col_own[1, g : g + 1, :] = to_lanes(jnp.sum(a * fac[gs, :], axis=1, keepdims=True))
    send_cols(1)
    wait_cols(col_recv, 1)
    tot = col_own[1]
    for j in range(ndp - 1):
        tot = tot + col_in[1, j]
    tot = (2.0**total_ratio) / tot
    for g in range(groups):
        gs = pl.ds(g * GROUP, GROUP)
        fac[gs, :] = fac[gs, :] * to_rows(tot[g : g + 1, :])

    row_pass(2)

    for g in range(groups):
        gs = pl.ds(g * GROUP, GROUP)
        f = fac[gs, :]

        def plan_step(i, a):
            x = (b[gs, tile(i)] * f) * pot[0:1, tile(i)]
            plan[gs, tile(i)] = x.astype(bf16)
            return a + x

        a = lax.fori_loop(0, tiles, plan_step, jnp.zeros((GROUP, LANES), f32), unroll=4)
        mass_own[g : g + 1, :] = to_lanes(jnp.sum(a, axis=1, keepdims=True))
    for o, (dz, dy) in enumerate(offsets):
        pltpu.make_async_remote_copy(
            src_ref=mass_own, dst_ref=mass_in.at[o], send_sem=mass_send, recv_sem=mass_recv,
            device_id={"dp": dp_peer(dz, dy)}, device_id_type=MESH,
        ).start()

    blk = 256 if width % 256 == 0 else width
    for j in range(width // blk):
        feats = pl.ds(j * blk, blk)
        s = nn_dot(plan[...], e[:, feats]).T
        sums[feats, :] = s
        low[feats, :] = s.astype(bf16)
    for o, (dz, dy) in enumerate(offsets):
        peer = dp_peer(dz, dy)
        pltpu.make_async_remote_copy(
            src_ref=low.at[pl.ds(pl.multiple_of(peer * own, own), own), :], dst_ref=rs_in.at[o],
            send_sem=rs_send, recv_sem=rs_recv, device_id={"dp": peer}, device_id_type=MESH,
        ).start()

    pltpu.make_async_copy(mass_in, mass_in, mass_recv).wait()
    mass = mass_own[...]
    for j in range(ndp - 1):
        mass = mass + mass_in[j]
    pltpu.make_async_copy(rs_in, rs_in, rs_recv).wait()
    for g in range(groups):
        gs = pl.ds(g * GROUP, GROUP)
        tot = sums[mine, gs]
        for j in range(ndp - 1):
            tot = tot + rs_in[j, :, gs].astype(f32)
        out_ref[:, gs] = tot / mass[g : g + 1, :]

    for h in range(HALVES):
        wait_ct(ct_send, h)
    for r in range(ROUNDS):
        for ch in range(chunks):
            wait_rows(row_send, r, ch)
    for r in range(ROUNDS - 1):
        wait_cols(col_send, r)
    pltpu.make_async_copy(mass_in, mass_in, mass_send).wait()
    pltpu.make_async_copy(rs_in, rs_in, rs_send).wait()


def body(embeddings, centroids):
    ndp, ncent = lax.axis_size("dp"), lax.axis_size("cent")
    n, width = embeddings.shape
    k, own = centroids.shape
    chunks = 2
    w = n // (8 * chunks)
    dma = pltpu.SemaphoreType.DMA
    out = pl.pallas_call(
        functools.partial(kernel, ndp, ncent, chunks),
        out_shape=jax.ShapeDtypeStruct((own, k), f32),
        in_specs=[pl.BlockSpec(memory_space=pl.ANY), pl.BlockSpec(memory_space=pltpu.VMEM)],
        out_specs=pl.BlockSpec(memory_space=pltpu.VMEM),
        scratch_shapes=[
            pltpu.VMEM((n, width), bf16),
            pltpu.VMEM((own, k), bf16),
            pltpu.VMEM((width, k), bf16),
            pltpu.VMEM((k, width), bf16),
            pltpu.VMEM((k, n), f32),
            pltpu.VMEM((k, n), bf16),
            pltpu.VMEM((width, k), f32),
            pltpu.VMEM((width, k), bf16),
            pltpu.VMEM((ROUNDS, chunks, 8, w), f32),
            pltpu.VMEM((ROUNDS, chunks, ncent - 1, 8, w), f32),
            pltpu.VMEM((8, n), f32),
            pltpu.VMEM((8, n), f32),
            pltpu.VMEM((ROUNDS - 1, k // GROUP, LANES), f32),
            pltpu.VMEM((ROUNDS - 1, ndp - 1, k // GROUP, LANES), f32),
            pltpu.VMEM((k // GROUP, LANES), f32),
            pltpu.VMEM((ndp - 1, k // GROUP, LANES), f32),
            pltpu.VMEM((k, LANES), f32),
            pltpu.VMEM((k, LANES), f32),
            pltpu.VMEM((ndp - 1, own, k), bf16),
            dma((E_PARTS,)),
            dma((HALVES,)),
            dma((HALVES,)),
            dma((ROUNDS, chunks)),
            dma((ROUNDS, chunks)),
            dma((ROUNDS - 1,)),
            dma((ROUNDS - 1,)),
            dma,
            dma,
            dma,
            dma,
        ],
        compiler_params=pltpu.CompilerParams(
            collective_id=0, has_side_effects=True, vmem_limit_bytes=60 * 2**20
        ),
        name="sinkhorn",
    )(embeddings, centroids)
    return out.T


def solution(mesh):
    return jax.shard_map(
        body,
        mesh=mesh,
        in_specs=(P("dp", None), P("cent", "dp")),
        out_specs=P("cent", "dp"),
        check_vma=False,
    )
```

```python
import functools
import math

import jax
import jax.numpy as jnp
from jax import lax
from jax.experimental import pallas as pl
from jax.experimental.pallas import tpu as pltpu
from jax.sharding import PartitionSpec as P

MESH = pl.DeviceIdType.MESH
f32 = jnp.float32
bf16 = jnp.bfloat16
LANES = 128
GROUP = 128
ROUNDS = 3
E_PARTS = 4
HALVES = 2


def nt_dot(a, b):
    return lax.dot_general(a, b, (((1,), (1,)), ((), ())), preferred_element_type=f32)


def nn_dot(a, b):
    return lax.dot_general(a, b, (((1,), (0,)), ((), ())), preferred_element_type=f32)


def lse2(parts):
    top = functools.reduce(jnp.maximum, parts)
    return top + jnp.log2(functools.reduce(jnp.add, [jnp.exp2(p - top) for p in parts]))


def to_lanes(col):
    return jnp.broadcast_to(col, (GROUP, LANES)).T[0:1, :]


def to_rows(row):
    return jnp.broadcast_to(row, (LANES, GROUP)).T


def kernel(
    ndp, ncent, chunks,
    e_hbm, c_hbm, out_ref,
    c_in, e, ct_own, ct, c, b, plan, sums, low,
    row_own, row_in, acc8, pot,
    col_own, col_in, mass_own, mass_in,
    peak, fac, part, rs_in,
    c_sem, e_sem, near_recv, ct_send, ct_recv, row_send, row_recv, col_send, col_recv,
    mass_send, mass_recv, rs_send, rs_recv,
):
    n, width = e.shape
    k = c.shape[0]
    own = width // ndp
    ny = math.isqrt(ndp)
    nz = ndp // ny
    w = n // (8 * chunks)
    groups = k // GROUP
    half = k // HALVES
    total_ratio = math.log2((n * ndp) / (k * ncent))

    pending = []

    me = lax.axis_index("dp")
    mec = lax.axis_index("cent")
    my_z, my_y = me // ny, me % ny

    offsets = [(dz, dy) for dz in range(nz) for dy in range(ny)][1:]

    def dp_peer(dz, dy):
        return ((my_z + dz) % nz) * ny + (my_y + dy) % ny

    def cent_peer(o):
        return (mec + o) % ncent

    barrier = pltpu.get_barrier_semaphore()
    for dz, dy in offsets:
        pl.semaphore_signal(barrier, inc=1, device_id={"dp": dp_peer(dz, dy)}, device_id_type=MESH)
    for o in range(1, ncent):
        pl.semaphore_signal(barrier, inc=1, device_id={"cent": cent_peer(o)}, device_id_type=MESH)

    c_copy = pltpu.make_async_copy(c_hbm, c_in, c_sem)
    c_copy.start()
    e_copies = []
    step = n // E_PARTS
    for i in range(E_PARTS):
        rows = pl.ds(i * step, step)
        e_copies.append(pltpu.make_async_copy(e_hbm.at[rows], e.at[rows], e_sem.at[i]))
        e_copies[-1].start()

    eye = (
        lax.broadcasted_iota(jnp.int32, (own, own), 0) == lax.broadcasted_iota(jnp.int32, (own, own), 1)
    ).astype(f32).astype(bf16)
    c_copy.wait()
    ct_own[...] = nt_dot(eye, c_in[...]).astype(bf16)

    def feats_of(dp):
        return pl.ds(pl.multiple_of(dp * own, own), own)

    mine = feats_of(me)
    ct[mine, :] = ct_own[...]

    pl.semaphore_wait(barrier, len(offsets) + ncent - 1)

    quarters = 2 * HALVES
    quart = k // quarters

    def line(q, first):
        if (q % 2 == 0) == first:
            return [(d, 0) for d in range(1, nz)]
        return [(0, d) for d in range(1, ny)]

    def send_ct(q, src, rows, off, sem):
        cols = pl.ds(q * quart, quart)
        pltpu.make_async_remote_copy(
            src_ref=src.at[:, cols] if src is ct_own else src.at[rows, cols], dst_ref=ct.at[rows, cols],
            send_sem=ct_send.at[q], recv_sem=sem,
            device_id={"dp": dp_peer(*off)}, device_id_type=MESH,
        ).start()

    def wait_ct(sem, q, blocks):
        part_ = ct.at[pl.ds(0, own * blocks), pl.ds(q * quart, quart)]
        pltpu.make_async_copy(part_, part_, sem).wait()

    for q in range(quarters):
        for j, off in enumerate(line(q, True)):
            send_ct(q, ct_own, mine, off, near_recv.at[q, j])
        for off in line(q, False):
            send_ct(q, ct_own, mine, off, ct_recv.at[q])
        pending.append(functools.partial(wait_ct, ct_send.at[q], q, ndp - 1))
    for q in range(quarters):
        near = line(q, True)
        order = sorted(range(len(near)), key=lambda j: min(j + 1, len(near) - j))
        for j in order:
            wait_ct(near_recv.at[q, len(near) - 1 - j], q, 1)
            for off in line(q, False):
                send_ct(q, ct, feats_of(dp_peer(*near[j])), off, ct_recv.at[q])

    unit = 4.0 / math.sqrt(width) / math.log(2.0)
    wide = 2 * w

    def send_rows(r, ch):
        for o in range(1, ncent):
            pltpu.make_async_remote_copy(
                src_ref=row_own.at[r, ch], dst_ref=row_in.at[r, ch, o - 1],
                send_sem=row_send.at[r, ch], recv_sem=row_recv.at[r, ch],
                device_id={"cent": cent_peer(o)}, device_id_type=MESH,
            ).start()
        pending.append(lambda: wait_rows(row_send, r, ch))

    def wait_rows(sem, r, ch):
        part_ = row_in.at[r, ch]
        pltpu.make_async_copy(part_, part_, sem.at[r, ch]).wait()

    for h in range(HALVES):
        for q in (2 * h, 2 * h + 1):
            wait_ct(ct_recv.at[q], q, ndp - 1 - len(line(q, True)))
        rows = pl.ds(h * half, half)
        c[rows, :] = ct[:, rows].T
        for ch in range(chunks):
            for i in range(0, 8, 2):
                at = (ch * 8 + i) * w
                toks = pl.ds(at, wide)
                if h == 0 and at % step == 0:
                    e_copies[at // step].wait()
                x = nt_dot(c[rows, :], e[toks, :]) * unit
                b[rows, toks] = x
                top = jnp.max(x, axis=0, keepdims=True)
                tot = jnp.sum(jnp.exp2(x - top), axis=0, keepdims=True)
                lse = top + jnp.log2(tot)
                if h == 0:
                    acc8[0:1, toks] = lse
                else:
                    lse = lse2([lse, acc8[0:1, toks]])
                    row_own[0, ch, i : i + 1, :] = lse[:, :w]
                    row_own[0, ch, i + 1 : i + 2, :] = lse[:, w:]
            if h == HALVES - 1:
                send_rows(0, ch)

    tiles = n // (chunks * LANES)

    def tile(ch, i):
        return pl.ds(pl.multiple_of((ch * tiles + i) * LANES, LANES), LANES)

    def over_tiles(f, init):
        return lax.fori_loop(0, tiles, f, init, unroll=tiles)

    def spread_rows(ch, dense):
        for i in range(8):
            pot[0:1, pl.ds((ch * 8 + i) * w, w)] = dense[i : i + 1, :]

    def send_cols(r):
        for o, (dz, dy) in enumerate(offsets):
            pltpu.make_async_remote_copy(
                src_ref=col_own.at[r], dst_ref=col_in.at[r, o],
                send_sem=col_send.at[r], recv_sem=col_recv.at[r],
                device_id={"dp": dp_peer(dz, dy)}, device_id_type=MESH,
            ).start()
        pending.append(lambda: wait_cols(col_send, r))

    def wait_cols(sem, r):
        part_ = col_in.at[r]
        pltpu.make_async_copy(part_, part_, sem.at[r]).wait()

    for ch in range(chunks):
        wait_rows(row_recv, 0, ch)
        spread_rows(ch, -lse2([row_own[0, ch]] + [row_in[0, ch, j] for j in range(ncent - 1)]))
        for g in range(groups):
            gs = pl.ds(g * GROUP, GROUP)

            def top_step(i, m):
                return jnp.maximum(m, b[gs, tile(ch, i)] + pot[0:1, tile(ch, i)])

            m = over_tiles(top_step, jnp.full((GROUP, LANES), -jnp.inf, f32))
            m = jnp.broadcast_to(jnp.max(m, axis=1, keepdims=True), (GROUP, LANES))
            peak[ch, gs, :] = m

            def exp_step(i, a):
                x = jnp.exp2((b[gs, tile(ch, i)] + pot[0:1, tile(ch, i)]) - m)
                b[gs, tile(ch, i)] = x
                return a + x

            a = over_tiles(exp_step, jnp.zeros((GROUP, LANES), f32))
            lse = to_lanes(m[:, 0:1] + jnp.log2(jnp.sum(a, axis=1, keepdims=True)))
            if ch > 0:
                lse = lse2([lse, col_own[0, g : g + 1, :]])
            col_own[0, g : g + 1, :] = lse
    send_cols(0)
    wait_cols(col_recv, 0)
    lse = lse2([col_own[0]] + [col_in[0, j] for j in range(ndp - 1)])
    for g in range(groups):
        gs = pl.ds(g * GROUP, GROUP)
        shift = total_ratio - to_rows(lse[g : g + 1, :])
        for ch in range(chunks):
            fac[ch, gs, :] = jnp.exp2(peak[ch, gs, :] + shift)

    def send_row_sums(r):
        for ch in range(chunks):
            for g in range(groups):
                gs = pl.ds(g * GROUP, GROUP)
                f = fac[ch, gs, :]

                def step_(i, _):
                    x = jnp.sum((b[gs, tile(ch, i)] * f).reshape(GROUP // 8, 8, LANES), axis=0)
                    if g > 0:
                        x = x + acc8[:, tile(ch, i)]
                    acc8[:, tile(ch, i)] = x
                    return 0

                over_tiles(step_, 0)
            for i in range(8):
                s = jnp.sum(acc8[:, pl.ds((ch * 8 + i) * w, w)], axis=0, keepdims=True)
                row_own[r, ch, i : i + 1, :] = s
            send_rows(r, ch)

    def take_row_sums(r, ch):
        wait_rows(row_recv, r, ch)
        dense = row_own[r, ch]
        for j in range(ncent - 1):
            dense = dense + row_in[r, ch, j]
        spread_rows(ch, 1.0 / dense)

    send_row_sums(1)
    for ch in range(chunks):
        take_row_sums(1, ch)
        for g in range(groups):
            gs = pl.ds(g * GROUP, GROUP)

            def col_step(i, a):
                return a + b[gs, tile(ch, i)] * pot[0:1, tile(ch, i)]

            a = over_tiles(col_step, jnp.zeros((GROUP, LANES), f32)) * fac[ch, gs, :]
            if ch > 0:
                a = a + part[gs, :]
            if ch < chunks - 1:
                part[gs, :] = a
            else:
                col_own[1, g : g + 1, :] = to_lanes(jnp.sum(a, axis=1, keepdims=True))
    send_cols(1)
    wait_cols(col_recv, 1)
    tot = col_own[1]
    for j in range(ndp - 1):
        tot = tot + col_in[1, j]
    tot = (2.0**total_ratio) / tot
    for g in range(groups):
        gs = pl.ds(g * GROUP, GROUP)
        scale = to_rows(tot[g : g + 1, :])
        for ch in range(chunks):
            fac[ch, gs, :] = fac[ch, gs, :] * scale

    send_row_sums(2)
    for ch in range(chunks):
        take_row_sums(2, ch)

    def make_plan(g):
        gs = pl.ds(g * GROUP, GROUP)
        a = jnp.zeros((GROUP, LANES), f32)
        for ch in range(chunks):
            f = fac[ch, gs, :]

            def plan_step(i, a):
                x = (b[gs, tile(ch, i)] * f) * pot[0:1, tile(ch, i)]
                plan[gs, tile(ch, i)] = x.astype(bf16)
                return a + x

            a = over_tiles(plan_step, a)
        mass_own[g : g + 1, :] = to_lanes(jnp.sum(a, axis=1, keepdims=True))

    def wait_sums(sem, g):
        part_ = rs_in.at[g]
        pltpu.make_async_copy(part_, part_, sem.at[g]).wait()

    make_plan(0)
    for g in range(groups):
        if g + 1 < groups:
            make_plan(g + 1)
        s = nn_dot(plan[pl.ds(g * GROUP, GROUP), :], e[...]).T
        sums[g] = s
        low[g] = s.astype(bf16)
        for o, (dz, dy) in enumerate(offsets):
            peer = dp_peer(dz, dy)
            pltpu.make_async_remote_copy(
                src_ref=low.at[g, feats_of(peer), :], dst_ref=rs_in.at[g, o],
                send_sem=rs_send.at[g], recv_sem=rs_recv.at[g],
                device_id={"dp": peer}, device_id_type=MESH,
            ).start()
        pending.append(functools.partial(wait_sums, rs_send, g))
        if g == max(groups - 2, 0):
            for o, (dz, dy) in enumerate(offsets):
                pltpu.make_async_remote_copy(
                    src_ref=mass_own, dst_ref=mass_in.at[o], send_sem=mass_send, recv_sem=mass_recv,
                    device_id={"dp": dp_peer(dz, dy)}, device_id_type=MESH,
                ).start()
            pending.append(lambda: pltpu.make_async_copy(mass_in, mass_in, mass_send).wait())

    pltpu.make_async_copy(mass_in, mass_in, mass_recv).wait()
    mass = mass_own[...]
    for j in range(ndp - 1):
        mass = mass + mass_in[j]
    for g in range(groups):
        wait_sums(rs_recv, g)
        tot = sums[g, mine, :]
        for j in range(ndp - 1):
            tot = tot + rs_in[g, j].astype(f32)
        out_ref[:, pl.ds(g * GROUP, GROUP)] = tot / mass[g : g + 1, :]

    for wait in pending:
        wait()


def body(embeddings, centroids):
    ndp, ncent = lax.axis_size("dp"), lax.axis_size("cent")
    n, width = embeddings.shape
    k, own = centroids.shape
    chunks = 2
    w = n // (8 * chunks)
    groups = k // GROUP
    line = math.isqrt(ndp)
    dma = pltpu.SemaphoreType.DMA
    out = pl.pallas_call(
        functools.partial(kernel, ndp, ncent, chunks),
        out_shape=jax.ShapeDtypeStruct((own, k), f32),
        in_specs=[pl.BlockSpec(memory_space=pl.ANY), pl.BlockSpec(memory_space=pl.ANY)],
        out_specs=pl.BlockSpec(memory_space=pltpu.VMEM),
        scratch_shapes=[
            pltpu.VMEM((k, own), bf16),
            pltpu.VMEM((n, width), bf16),
            pltpu.VMEM((own, k), bf16),
            pltpu.VMEM((width, k), bf16),
            pltpu.VMEM((k, width), bf16),
            pltpu.VMEM((k, n), f32),
            pltpu.VMEM((k, n), bf16),
            pltpu.VMEM((groups, width, GROUP), f32),
            pltpu.VMEM((groups, width, GROUP), bf16),
            pltpu.VMEM((ROUNDS, chunks, 8, w), f32),
            pltpu.VMEM((ROUNDS, chunks, ncent - 1, 8, w), f32),
            pltpu.VMEM((8, n), f32),
            pltpu.VMEM((8, n), f32),
            pltpu.VMEM((ROUNDS - 1, groups, LANES), f32),
            pltpu.VMEM((ROUNDS - 1, ndp - 1, groups, LANES), f32),
            pltpu.VMEM((groups, LANES), f32),
            pltpu.VMEM((ndp - 1, groups, LANES), f32),
            pltpu.VMEM((chunks, k, LANES), f32),
            pltpu.VMEM((chunks, k, LANES), f32),
            pltpu.VMEM((k, LANES), f32),
            pltpu.VMEM((groups, ndp - 1, own, GROUP), bf16),
            dma,
            dma((E_PARTS,)),
            dma((2 * HALVES, line - 1)),
            dma((2 * HALVES,)),
            dma((2 * HALVES,)),
            dma((ROUNDS, chunks)),
            dma((ROUNDS, chunks)),
            dma((ROUNDS - 1,)),
            dma((ROUNDS - 1,)),
            dma,
            dma,
            dma((groups,)),
            dma((groups,)),
        ],
        compiler_params=pltpu.CompilerParams(
            collective_id=0, has_side_effects=True, vmem_limit_bytes=60 * 2**20
        ),
        name="sinkhorn",
    )(embeddings, centroids)
    return out.T


def solution(mesh):
    return jax.shard_map(
        body,
        mesh=mesh,
        in_specs=(P("dp", None), P("cent", "dp")),
        out_specs=P("cent", "dp"),
        check_vma=False,
    )
```

```python
import functools
import math

import jax
import jax.numpy as jnp
from jax import lax
from jax.experimental import pallas as pl
from jax.experimental.pallas import tpu as pltpu
from jax.sharding import PartitionSpec as P

MESH = pl.DeviceIdType.MESH
f32 = jnp.float32
bf16 = jnp.bfloat16
LANES = 128
GROUP = 128
ROUNDS = 3
E_PARTS = 4
HALVES = 2


def nt_dot(a, b):
    return lax.dot_general(a, b, (((1,), (1,)), ((), ())), preferred_element_type=f32)


def nn_dot(a, b):
    return lax.dot_general(a, b, (((1,), (0,)), ((), ())), preferred_element_type=f32)


def lse2(parts):
    top = functools.reduce(jnp.maximum, parts)
    return top + jnp.log2(functools.reduce(jnp.add, [jnp.exp2(p - top) for p in parts]))


def to_lanes(col):
    return jnp.broadcast_to(col, (GROUP, LANES)).T[0:1, :]


def to_rows(row):
    return jnp.broadcast_to(row, (LANES, GROUP)).T


def kernel(
    ndp, ncent, chunks,
    e_hbm, c_hbm, out_ref,
    e, ct_own, ct, c, b, plan, sums, low,
    row_own, row_in, acc8, pot,
    col_own, col_in, mass_own, mass_in,
    peak, fac, part, rs_in,
    c_sem, e_sem, near_recv, ct_send, ct_recv, row_send, row_recv, col_send, col_recv,
    mass_send, mass_recv, rs_send, rs_recv,
):
    n, width = e.shape
    k = c.shape[0]
    own = width // ndp
    ny = math.isqrt(ndp)
    nz = ndp // ny
    w = n // (8 * chunks)
    groups = k // GROUP
    half = k // HALVES
    total_ratio = math.log2((n * ndp) / (k * ncent))

    pending = []

    me = lax.axis_index("dp")
    mec = lax.axis_index("cent")
    my_z, my_y = me // ny, me % ny

    offsets = [(dz, dy) for dz in range(nz) for dy in range(ny)][1:]

    def dp_peer(dz, dy):
        return ((my_z + dz) % nz) * ny + (my_y + dy) % ny

    def cent_peer(o):
        return (mec + o) % ncent

    barrier = pltpu.get_barrier_semaphore()
    for dz, dy in offsets:
        pl.semaphore_signal(barrier, inc=1, device_id={"dp": dp_peer(dz, dy)}, device_id_type=MESH)
    for o in range(1, ncent):
        pl.semaphore_signal(barrier, inc=1, device_id={"cent": cent_peer(o)}, device_id_type=MESH)

    c_copy = pltpu.make_async_copy(c_hbm, ct_own, c_sem)
    c_copy.start()
    e_copies = []
    step = n // E_PARTS
    for i in range(E_PARTS):
        rows = pl.ds(i * step, step)
        e_copies.append(pltpu.make_async_copy(e_hbm.at[rows], e.at[rows], e_sem.at[i]))
        e_copies[-1].start()

    c_copy.wait()

    def feats_of(dp):
        return pl.ds(pl.multiple_of(dp * own, own), own)

    mine = feats_of(me)
    ct[mine, :] = ct_own[...]

    pl.semaphore_wait(barrier, len(offsets) + ncent - 1)

    def hops(d, size):
        return min(d, size - d)

    def routes(dz, dy):
        a, b_ = hops(dz, nz), hops(dy, ny)
        if a == b_ and a > 1:
            return (0, half // 2), (half // 2, half)
        if a > b_ or (a == b_ and dz == dy):
            return (0, half), None
        return None, (0, half)

    def send_ct(h, src, rows, part_, off, sem):
        cols = pl.ds(h * half + part_[0], part_[1] - part_[0])
        pltpu.make_async_remote_copy(
            src_ref=ct_own.at[:, cols] if src is ct_own else src.at[rows, cols], dst_ref=ct.at[rows, cols],
            send_sem=ct_send.at[h], recv_sem=sem,
            device_id={"dp": dp_peer(*off)}, device_id_type=MESH,
        ).start()

    def wait_ct(sem, h, blocks):
        part_ = ct.at[pl.ds(0, own * blocks), pl.ds(h * half, half)]
        pltpu.make_async_copy(part_, part_, sem).wait()

    lines = [(d, 0) for d in range(1, nz)] + [(0, d) for d in range(1, ny)]
    far_first = sorted(lines, key=lambda o: -hops(o[0], nz) - hops(o[1], ny))
    for h in range(HALVES):
        for off in far_first:
            send_ct(h, ct_own, mine, (0, half), off, near_recv.at[h, lines.index(off)])
        pending.append(functools.partial(wait_ct, ct_send.at[h], h, ndp - 1))
    for h in range(HALVES):
        for dz, dy in far_first[::-1]:
            wait_ct(near_recv.at[h, lines.index((dz, dy))], h, 1)
            rows = feats_of(dp_peer(nz - dz, ny - dy))
            for d in range(1, ny if dy == 0 else nz):
                off, both = ((0, d), (dz, d)) if dy == 0 else ((d, 0), (d, dy))
                part_ = routes(*both)[0 if dy == 0 else 1]
                if part_:
                    send_ct(h, ct, rows, part_, off, ct_recv.at[h])

    unit = 4.0 / math.sqrt(width) / math.log(2.0)
    wide = 2 * w

    def send_rows(r, ch):
        for o in range(1, ncent):
            pltpu.make_async_remote_copy(
                src_ref=row_own.at[r, ch], dst_ref=row_in.at[r, ch, o - 1],
                send_sem=row_send.at[r, ch], recv_sem=row_recv.at[r, ch],
                device_id={"cent": cent_peer(o)}, device_id_type=MESH,
            ).start()
        pending.append(lambda: wait_rows(row_send, r, ch))

    def wait_rows(sem, r, ch):
        part_ = row_in.at[r, ch]
        pltpu.make_async_copy(part_, part_, sem.at[r, ch]).wait()

    for copy in e_copies:
        copy.wait()
    for h in range(HALVES):
        wait_ct(ct_recv.at[h], h, ndp - 1 - len(lines))
        rows = pl.ds(h * half, half)
        c[rows, :] = ct[:, rows].T
        for ch in range(chunks):
            for i in range(0, 8, 2):
                at = (ch * 8 + i) * w
                toks = pl.ds(at, wide)
                x = nt_dot(c[rows, :], e[toks, :]) * unit
                b[rows, toks] = x
                top = jnp.max(x, axis=0, keepdims=True)
                tot = jnp.sum(jnp.exp2(x - top), axis=0, keepdims=True)
                lse = top + jnp.log2(tot)
                if h == 0:
                    acc8[0:1, toks] = lse
                else:
                    lse = lse2([lse, acc8[0:1, toks]])
                    row_own[0, ch, i : i + 1, :] = lse[:, :w]
                    row_own[0, ch, i + 1 : i + 2, :] = lse[:, w:]
            if h == HALVES - 1:
                send_rows(0, ch)

    tiles = n // (chunks * LANES)

    def tile(ch, i):
        return pl.ds(pl.multiple_of((ch * tiles + i) * LANES, LANES), LANES)

    def over_tiles(f, init):
        return lax.fori_loop(0, tiles, f, init, unroll=tiles)

    def spread_rows(ch, dense):
        for i in range(8):
            pot[0:1, pl.ds((ch * 8 + i) * w, w)] = dense[i : i + 1, :]

    def send_cols(r):
        for o, (dz, dy) in enumerate(offsets):
            pltpu.make_async_remote_copy(
                src_ref=col_own.at[r], dst_ref=col_in.at[r, o],
                send_sem=col_send.at[r], recv_sem=col_recv.at[r],
                device_id={"dp": dp_peer(dz, dy)}, device_id_type=MESH,
            ).start()
        pending.append(lambda: wait_cols(col_send, r))

    def wait_cols(sem, r):
        part_ = col_in.at[r]
        pltpu.make_async_copy(part_, part_, sem.at[r]).wait()

    for ch in range(chunks):
        wait_rows(row_recv, 0, ch)
        spread_rows(ch, -lse2([row_own[0, ch]] + [row_in[0, ch, j] for j in range(ncent - 1)]))
        for g in range(groups):
            gs = pl.ds(g * GROUP, GROUP)

            def top_step(i, m):
                return jnp.maximum(m, b[gs, tile(ch, i)] + pot[0:1, tile(ch, i)])

            m = over_tiles(top_step, jnp.full((GROUP, LANES), -jnp.inf, f32))
            m = jnp.broadcast_to(jnp.max(m, axis=1, keepdims=True), (GROUP, LANES))
            peak[ch, gs, :] = m

            def exp_step(i, a):
                x = jnp.exp2((b[gs, tile(ch, i)] + pot[0:1, tile(ch, i)]) - m)
                b[gs, tile(ch, i)] = x
                return a + x

            a = over_tiles(exp_step, jnp.zeros((GROUP, LANES), f32))
            lse = to_lanes(m[:, 0:1] + jnp.log2(jnp.sum(a, axis=1, keepdims=True)))
            if ch > 0:
                lse = lse2([lse, col_own[0, g : g + 1, :]])
            col_own[0, g : g + 1, :] = lse
    send_cols(0)
    wait_cols(col_recv, 0)
    lse = lse2([col_own[0]] + [col_in[0, j] for j in range(ndp - 1)])
    for g in range(groups):
        gs = pl.ds(g * GROUP, GROUP)
        shift = total_ratio - to_rows(lse[g : g + 1, :])
        for ch in range(chunks):
            fac[ch, gs, :] = jnp.exp2(peak[ch, gs, :] + shift)

    def send_row_sums(r):
        for ch in range(chunks):
            for g in range(groups):
                gs = pl.ds(g * GROUP, GROUP)
                f = fac[ch, gs, :]

                def step_(i, _):
                    x = jnp.sum((b[gs, tile(ch, i)] * f).reshape(GROUP // 8, 8, LANES), axis=0)
                    if g > 0:
                        x = x + acc8[:, tile(ch, i)]
                    acc8[:, tile(ch, i)] = x
                    return 0

                over_tiles(step_, 0)
            for i in range(8):
                s = jnp.sum(acc8[:, pl.ds((ch * 8 + i) * w, w)], axis=0, keepdims=True)
                row_own[r, ch, i : i + 1, :] = s
            send_rows(r, ch)

    def take_row_sums(r, ch):
        wait_rows(row_recv, r, ch)
        dense = row_own[r, ch]
        for j in range(ncent - 1):
            dense = dense + row_in[r, ch, j]
        spread_rows(ch, 1.0 / dense)

    send_row_sums(1)
    for ch in range(chunks):
        take_row_sums(1, ch)
        for g in range(groups):
            gs = pl.ds(g * GROUP, GROUP)

            def col_step(i, a):
                return a + b[gs, tile(ch, i)] * pot[0:1, tile(ch, i)]

            a = over_tiles(col_step, jnp.zeros((GROUP, LANES), f32)) * fac[ch, gs, :]
            if ch > 0:
                a = a + part[gs, :]
            if ch < chunks - 1:
                part[gs, :] = a
            else:
                col_own[1, g : g + 1, :] = to_lanes(jnp.sum(a, axis=1, keepdims=True))
    send_cols(1)
    wait_cols(col_recv, 1)
    tot = col_own[1]
    for j in range(ndp - 1):
        tot = tot + col_in[1, j]
    tot = (2.0**total_ratio) / tot
    for g in range(groups):
        gs = pl.ds(g * GROUP, GROUP)
        scale = to_rows(tot[g : g + 1, :])
        for ch in range(chunks):
            fac[ch, gs, :] = fac[ch, gs, :] * scale

    send_row_sums(2)
    for ch in range(chunks):
        take_row_sums(2, ch)

    def make_plan(g):
        gs = pl.ds(g * GROUP, GROUP)
        a = jnp.zeros((GROUP, LANES), f32)
        for ch in range(chunks):
            f = fac[ch, gs, :]

            def plan_step(i, a):
                x = (b[gs, tile(ch, i)] * f) * pot[0:1, tile(ch, i)]
                plan[gs, tile(ch, i)] = x.astype(bf16)
                return a + x

            a = over_tiles(plan_step, a)
        mass_own[g : g + 1, :] = to_lanes(jnp.sum(a, axis=1, keepdims=True))

    def wait_sums(sem, g):
        part_ = rs_in.at[g]
        pltpu.make_async_copy(part_, part_, sem.at[g]).wait()

    make_plan(0)
    for g in range(groups):
        if g + 1 < groups:
            make_plan(g + 1)
        s = nn_dot(plan[pl.ds(g * GROUP, GROUP), :], e[...]).T
        sums[g] = s
        low[g] = s.astype(bf16)
        for o, (dz, dy) in enumerate(offsets):
            peer = dp_peer(dz, dy)
            pltpu.make_async_remote_copy(
                src_ref=low.at[g, feats_of(peer), :], dst_ref=rs_in.at[g, o],
                send_sem=rs_send.at[g], recv_sem=rs_recv.at[g],
                device_id={"dp": peer}, device_id_type=MESH,
            ).start()
        pending.append(functools.partial(wait_sums, rs_send, g))
        if g == max(groups - 2, 0):
            for o, (dz, dy) in enumerate(offsets):
                pltpu.make_async_remote_copy(
                    src_ref=mass_own, dst_ref=mass_in.at[o], send_sem=mass_send, recv_sem=mass_recv,
                    device_id={"dp": dp_peer(dz, dy)}, device_id_type=MESH,
                ).start()
            pending.append(lambda: pltpu.make_async_copy(mass_in, mass_in, mass_send).wait())

    pltpu.make_async_copy(mass_in, mass_in, mass_recv).wait()
    mass = mass_own[...]
    for j in range(ndp - 1):
        mass = mass + mass_in[j]
    for g in range(groups):
        wait_sums(rs_recv, g)
        tot = sums[g, mine, :]
        for j in range(ndp - 1):
            tot = tot + rs_in[g, j].astype(f32)
        out_ref[:, pl.ds(g * GROUP, GROUP)] = tot / mass[g : g + 1, :]

    for wait in pending:
        wait()


def body(embeddings, centroids):
    centroids = centroids.T
    embeddings = pltpu.with_memory_space_constraint(embeddings, pltpu.HBM)
    centroids = pltpu.with_memory_space_constraint(centroids, pltpu.HBM)
    ndp, ncent = lax.axis_size("dp"), lax.axis_size("cent")
    n, width = embeddings.shape
    own, k = centroids.shape
    chunks = 2
    w = n // (8 * chunks)
    groups = k // GROUP
    line = math.isqrt(ndp)
    dma = pltpu.SemaphoreType.DMA
    out = pl.pallas_call(
        functools.partial(kernel, ndp, ncent, chunks),
        out_shape=pltpu.VMEM((own, k), f32),
        in_specs=[pl.BlockSpec(memory_space=pl.ANY), pl.BlockSpec(memory_space=pl.ANY)],
        out_specs=pl.BlockSpec(memory_space=pltpu.VMEM),
        scratch_shapes=[
            pltpu.VMEM((n, width), bf16),
            pltpu.VMEM((own, k), bf16),
            pltpu.VMEM((width, k), bf16),
            pltpu.VMEM((k, width), bf16),
            pltpu.VMEM((k, n), f32),
            pltpu.VMEM((k, n), bf16),
            pltpu.VMEM((groups, width, GROUP), f32),
            pltpu.VMEM((groups, width, GROUP), bf16),
            pltpu.VMEM((ROUNDS, chunks, 8, w), f32),
            pltpu.VMEM((ROUNDS, chunks, ncent - 1, 8, w), f32),
            pltpu.VMEM((8, n), f32),
            pltpu.VMEM((8, n), f32),
            pltpu.VMEM((ROUNDS - 1, groups, LANES), f32),
            pltpu.VMEM((ROUNDS - 1, ndp - 1, groups, LANES), f32),
            pltpu.VMEM((groups, LANES), f32),
            pltpu.VMEM((ndp - 1, groups, LANES), f32),
            pltpu.VMEM((chunks, k, LANES), f32),
            pltpu.VMEM((chunks, k, LANES), f32),
            pltpu.VMEM((k, LANES), f32),
            pltpu.VMEM((groups, ndp - 1, own, GROUP), bf16),
            dma,
            dma((E_PARTS,)),
            dma((HALVES, 2 * (line - 1))),
            dma((HALVES,)),
            dma((HALVES,)),
            dma((ROUNDS, chunks)),
            dma((ROUNDS, chunks)),
            dma((ROUNDS - 1,)),
            dma((ROUNDS - 1,)),
            dma,
            dma,
            dma((groups,)),
            dma((groups,)),
        ],
        compiler_params=pltpu.CompilerParams(
            collective_id=0, has_side_effects=True, vmem_limit_bytes=50 * 2**20
        ),
        name="sinkhorn",
    )(embeddings, centroids)
    return out.T


def solution(mesh):
    return jax.shard_map(
        body,
        mesh=mesh,
        in_specs=(P("dp", None), P("cent", "dp")),
        out_specs=P("cent", "dp"),
        check_vma=False,
    )
```

```python
import functools
import math

import jax
import jax.numpy as jnp
from jax import lax
from jax.experimental import pallas as pl
from jax.experimental.pallas import tpu as pltpu
from jax.sharding import PartitionSpec as P

MESH = pl.DeviceIdType.MESH
f32 = jnp.float32
bf16 = jnp.bfloat16
LANES = 128
GROUP = 128
ROUNDS = 3
E_PARTS = 4
HALVES = 2


def nt_dot(a, b):
    return lax.dot_general(a, b, (((1,), (1,)), ((), ())), preferred_element_type=f32)


def nn_dot(a, b):
    return lax.dot_general(a, b, (((1,), (0,)), ((), ())), preferred_element_type=f32)


def lse2(parts):
    top = functools.reduce(jnp.maximum, parts)
    return top + jnp.log2(functools.reduce(jnp.add, [jnp.exp2(p - top) for p in parts]))


def lane_sums(a):
    return jnp.sum(a.T, axis=0, keepdims=True)


def to_rows(row):
    return jnp.broadcast_to(row, (LANES, GROUP)).T


def kernel(
    ndp, ncent, chunks,
    e_hbm, c_hbm, out_ref,
    e, ct_own, ct, c, b, plan, sums, low,
    row_own, row_in, acc8, pot,
    col_own, col_in, mass_own, mass_in,
    peak, fac, part, diag_in, line_out, line_in,
    c_sem, e_sem, near_recv, ct_send, ct_recv, row_send, row_recv, col_send, col_recv,
    mass_send, mass_recv, diag_send, diag_recv, line_send, line_recv,
):
    n, width = e.shape
    k = c.shape[0]
    own = width // ndp
    ny = math.isqrt(ndp)
    nz = ndp // ny
    w = n // (8 * chunks)
    groups = k // GROUP
    half = k // HALVES
    total_ratio = math.log2((n * ndp) / (k * ncent))

    pending = []

    me = lax.axis_index("dp")
    mec = lax.axis_index("cent")
    my_z, my_y = me // ny, me % ny

    def hops(d, size):
        return min(d, size - d)

    offsets = [(dz, dy) for dz in range(nz) for dy in range(ny)][1:]
    offsets.sort(key=lambda o: -hops(o[0], nz) - hops(o[1], ny))
    nx = ncent // 2
    cent_offsets = [(dx, core) for dx in range(nx) for core in range(2)][1:]
    cent_offsets.sort(key=lambda o: -hops(o[0], nx))

    def dp_peer(dz, dy):
        return ((my_z + dz) % nz) * ny + (my_y + dy) % ny

    def cent_peer(dx, core):
        return ((mec // 2 + dx) % nx) * 2 + (mec + core) % 2

    c_copy = pltpu.make_async_copy(c_hbm, ct_own, c_sem)
    c_copy.start()
    barrier = pltpu.get_barrier_semaphore()
    for dz, dy in offsets:
        pl.semaphore_signal(barrier, inc=1, device_id={"dp": dp_peer(dz, dy)}, device_id_type=MESH)
    for o in cent_offsets:
        pl.semaphore_signal(barrier, inc=1, device_id={"cent": cent_peer(*o)}, device_id_type=MESH)

    e_copies = []
    step = n // E_PARTS
    for i in range(E_PARTS):
        rows = pl.ds(i * step, step)
        e_copies.append(pltpu.make_async_copy(e_hbm.at[rows], e.at[rows], e_sem.at[i]))
        e_copies[-1].start()

    c_copy.wait()

    def feats_of(dp):
        return pl.ds(pl.multiple_of(dp * own, own), own)

    mine = feats_of(me)
    ct[mine, :] = ct_own[...]

    pl.semaphore_wait(barrier, len(offsets) + ncent - 1)

    def routes(dz, dy):
        a, b_ = hops(dz, nz), hops(dy, ny)
        if a == b_ and a > 1:
            return (0, half // 2), (half // 2, half)
        if a > b_ or (a == b_ and dz == dy):
            return (0, half), None
        return None, (0, half)

    def send_ct(h, src, rows, part_, off, sem):
        cols = pl.ds(h * half + part_[0], part_[1] - part_[0])
        pltpu.make_async_remote_copy(
            src_ref=ct_own.at[:, cols] if src is ct_own else src.at[rows, cols], dst_ref=ct.at[rows, cols],
            send_sem=ct_send.at[h], recv_sem=sem,
            device_id={"dp": dp_peer(*off)}, device_id_type=MESH,
        ).start()

    def wait_ct(sem, h, blocks):
        part_ = ct.at[pl.ds(0, own * blocks), pl.ds(h * half, half)]
        pltpu.make_async_copy(part_, part_, sem).wait()

    lines = [(d, 0) for d in range(1, nz)] + [(0, d) for d in range(1, ny)]
    far_first = sorted(lines, key=lambda o: -hops(o[0], nz) - hops(o[1], ny))
    for h in range(HALVES):
        for off in far_first:
            send_ct(h, ct_own, mine, (0, half), off, near_recv.at[h, lines.index(off)])
        pending.append(functools.partial(wait_ct, ct_send.at[h], h, ndp - 1))
    for h in range(HALVES):
        for dz, dy in far_first[::-1]:
            wait_ct(near_recv.at[h, lines.index((dz, dy))], h, 1)
            rows = feats_of(dp_peer(nz - dz, ny - dy))
            for d in range(1, ny if dy == 0 else nz):
                off, both = ((0, d), (dz, d)) if dy == 0 else ((d, 0), (d, dy))
                part_ = routes(*both)[0 if dy == 0 else 1]
                if part_:
                    send_ct(h, ct, rows, part_, off, ct_recv.at[h])

    unit = 4.0 / math.sqrt(width) / math.log(2.0)
    wide = 2 * w

    def send_rows(r, ch):
        for j, o in enumerate(cent_offsets):
            pltpu.make_async_remote_copy(
                src_ref=row_own.at[r, ch], dst_ref=row_in.at[r, ch, j],
                send_sem=row_send.at[r, ch], recv_sem=row_recv.at[r, ch],
                device_id={"cent": cent_peer(*o)}, device_id_type=MESH,
            ).start()
        pending.append(lambda: wait_rows(row_send, r, ch))

    def wait_rows(sem, r, ch):
        part_ = row_in.at[r, ch]
        pltpu.make_async_copy(part_, part_, sem.at[r, ch]).wait()

    for copy in e_copies:
        copy.wait()
    for h in range(HALVES):
        wait_ct(ct_recv.at[h], h, ndp - 1 - len(lines))
        rows = pl.ds(h * half, half)
        c[rows, :] = ct[:, rows].T
        for ch in range(chunks):
            for i in range(0, 8, 2):
                at = (ch * 8 + i) * w
                toks = pl.ds(at, wide)
                x = nt_dot(c[rows, :], e[toks, :]) * unit
                b[rows, toks] = x
                top = jnp.max(x, axis=0, keepdims=True)
                tot = jnp.sum(jnp.exp2(x - top), axis=0, keepdims=True)
                lse = top + jnp.log2(tot)
                if h == 0:
                    acc8[0:1, toks] = lse
                else:
                    lse = lse2([lse, acc8[0:1, toks]])
                    row_own[0, ch, i : i + 1, :] = lse[:, :w]
                    row_own[0, ch, i + 1 : i + 2, :] = lse[:, w:]
            if h == HALVES - 1:
                send_rows(0, ch)

    tiles = n // (chunks * LANES)

    def tile(ch, i):
        return pl.ds(pl.multiple_of((ch * tiles + i) * LANES, LANES), LANES)

    def over_tiles(f, init):
        return lax.fori_loop(0, tiles, f, init, unroll=tiles)

    def spread_rows(ch, dense):
        for i in range(8):
            pot[0:1, pl.ds((ch * 8 + i) * w, w)] = dense[i : i + 1, :]

    def send_cols(r):
        for o, (dz, dy) in enumerate(offsets):
            pltpu.make_async_remote_copy(
                src_ref=col_own.at[r], dst_ref=col_in.at[r, o],
                send_sem=col_send.at[r], recv_sem=col_recv.at[r],
                device_id={"dp": dp_peer(dz, dy)}, device_id_type=MESH,
            ).start()
        pending.append(lambda: wait_cols(col_send, r))

    def wait_cols(sem, r):
        part_ = col_in.at[r]
        pltpu.make_async_copy(part_, part_, sem.at[r]).wait()

    for ch in range(chunks):
        wait_rows(row_recv, 0, ch)
        spread_rows(ch, -lse2([row_own[0, ch]] + [row_in[0, ch, j] for j in range(ncent - 1)]))
        for g in range(groups):
            gs = pl.ds(g * GROUP, GROUP)

            def top_step(i, m):
                return jnp.maximum(m, b[gs, tile(ch, i)] + pot[0:1, tile(ch, i)])

            m = over_tiles(top_step, jnp.full((GROUP, LANES), -jnp.inf, f32))
            m = jnp.broadcast_to(jnp.max(m, axis=1, keepdims=True), (GROUP, LANES))
            peak[ch, gs, :] = m

            def exp_step(i, a):
                x = jnp.exp2((b[gs, tile(ch, i)] + pot[0:1, tile(ch, i)]) - m)
                b[gs, tile(ch, i)] = x
                return a + x

            a = over_tiles(exp_step, jnp.zeros((GROUP, LANES), f32))
            lse = m.T[0:1, :] + jnp.log2(lane_sums(a))
            if ch > 0:
                lse = lse2([lse, col_own[0, g : g + 1, :]])
            col_own[0, g : g + 1, :] = lse
    send_cols(0)
    wait_cols(col_recv, 0)
    lse = lse2([col_own[0]] + [col_in[0, j] for j in range(ndp - 1)])
    for g in range(groups):
        gs = pl.ds(g * GROUP, GROUP)
        shift = total_ratio - to_rows(lse[g : g + 1, :])
        for ch in range(chunks):
            fac[ch, gs, :] = jnp.exp2(peak[ch, gs, :] + shift)

    def send_row_sums(r):
        for ch in range(chunks):
            for g in range(groups):
                gs = pl.ds(g * GROUP, GROUP)
                f = fac[ch, gs, :]

                def step_(i, _):
                    x = jnp.sum((b[gs, tile(ch, i)] * f).reshape(GROUP // 8, 8, LANES), axis=0)
                    if g > 0:
                        x = x + acc8[:, tile(ch, i)]
                    acc8[:, tile(ch, i)] = x
                    return 0

                over_tiles(step_, 0)
            for i in range(8):
                s = jnp.sum(acc8[:, pl.ds((ch * 8 + i) * w, w)], axis=0, keepdims=True)
                row_own[r, ch, i : i + 1, :] = s
            send_rows(r, ch)

    def take_row_sums(r, ch):
        wait_rows(row_recv, r, ch)
        dense = row_own[r, ch]
        for j in range(ncent - 1):
            dense = dense + row_in[r, ch, j]
        spread_rows(ch, 1.0 / dense)

    send_row_sums(1)
    for ch in range(chunks):
        take_row_sums(1, ch)
        for g in range(groups):
            gs = pl.ds(g * GROUP, GROUP)

            def col_step(i, a):
                return a + b[gs, tile(ch, i)] * pot[0:1, tile(ch, i)]

            a = over_tiles(col_step, jnp.zeros((GROUP, LANES), f32)) * fac[ch, gs, :]
            if ch > 0:
                a = a + part[gs, :]
            if ch < chunks - 1:
                part[gs, :] = a
            else:
                col_own[1, g : g + 1, :] = lane_sums(a)
    send_cols(1)
    wait_cols(col_recv, 1)
    tot = col_own[1]
    for j in range(ndp - 1):
        tot = tot + col_in[1, j]
    tot = (2.0**total_ratio) / tot
    for g in range(groups):
        gs = pl.ds(g * GROUP, GROUP)
        scale = to_rows(tot[g : g + 1, :])
        for ch in range(chunks):
            fac[ch, gs, :] = fac[ch, gs, :] * scale

    def make_plan(ch, g):
        gs = pl.ds(g * GROUP, GROUP)
        f = fac[ch, gs, :]

        def plan_step(i, a):
            x = (b[gs, tile(ch, i)] * f) * pot[0:1, tile(ch, i)]
            plan[gs, tile(ch, i)] = x.astype(bf16)
            return a + x

        a = over_tiles(plan_step, jnp.zeros((GROUP, LANES), f32))
        if ch > 0:
            a = a + part[gs, :]
        if ch < chunks - 1:
            part[gs, :] = a
        else:
            mass_own[g : g + 1, :] = lane_sums(a)

    send_row_sums(2)
    for ch in range(chunks):
        take_row_sums(2, ch)
        for g in range(groups if ch < chunks - 1 else 1):
            make_plan(ch, g)

    def wait_all(buf, sem):
        pltpu.make_async_copy(buf, buf, sem).wait()

    diag = [o for o in offsets if o[0] and o[1]]

    def by_z(g, dz, dy):
        a, b_ = hops(dz, nz), hops(dy, ny)
        if a == b_:
            return dz == dy if a == 1 else g % 2 == 0
        return a < b_

    def send_sums(src, dst, sems, g, peer):
        pltpu.make_async_remote_copy(
            src_ref=src, dst_ref=dst, send_sem=sems[0].at[g], recv_sem=sems[1].at[g],
            device_id={"dp": peer}, device_id_type=MESH,
        ).start()

    def start_sums(g):
        for j, (dz, dy) in enumerate(diag):
            there = dp_peer(dz, 0) if by_z(g, dz, dy) else dp_peer(0, dy)
            send_sums(low.at[g, feats_of(dp_peer(dz, dy)), :], diag_in.at[g, j], (diag_send, diag_recv), g, there)
        pending.append(functools.partial(wait_all, diag_in.at[g], diag_send.at[g]))

    def pass_sums(g):
        wait_all(diag_in.at[g], diag_recv.at[g])
        for j, off in enumerate(far_first):
            peer = dp_peer(*off)
            tot = sums[g, feats_of(peer), :]
            for i, (dz, dy) in enumerate(diag):
                if off == ((0, dy) if by_z(g, dz, dy) else (dz, 0)):
                    tot = tot + diag_in[g, i].astype(f32)
            line_out[g, j] = tot
            send_sums(line_out.at[g, j], line_in.at[g, j], (line_send, line_recv), g, peer)

    for g in range(groups):
        if g + 1 < groups:
            make_plan(chunks - 1, g + 1)
        s = nn_dot(plan[pl.ds(g * GROUP, GROUP), :], e[...]).T
        sums[g] = s
        low[g] = s.astype(bf16)
        start_sums(g)
        if g == max(groups - 2, 0):
            for o, (dz, dy) in enumerate(offsets):
                pltpu.make_async_remote_copy(
                    src_ref=mass_own, dst_ref=mass_in.at[o], send_sem=mass_send, recv_sem=mass_recv,
                    device_id={"dp": dp_peer(dz, dy)}, device_id_type=MESH,
                ).start()
            pending.append(lambda: wait_all(mass_in, mass_send))
    for g in range(groups):
        pass_sums(g)

    for wait in pending:
        wait()

    wait_all(mass_in, mass_recv)
    mass = mass_own[...]
    for j in range(ndp - 1):
        mass = mass + mass_in[j]
    for g in range(groups):
        tot = sums[g, mine, :]
        wait_all(line_in.at[g], line_recv.at[g])
        for j in range(len(lines)):
            tot = tot + line_in[g, j]
        out_ref[:, pl.ds(g * GROUP, GROUP)] = tot / mass[g : g + 1, :]
    for g in range(groups):
        wait_all(line_in.at[g], line_send.at[g])


def body(embeddings, centroids):
    centroids = centroids.T
    embeddings = pltpu.with_memory_space_constraint(embeddings, pltpu.HBM)
    centroids = pltpu.with_memory_space_constraint(centroids, pltpu.HBM)
    ndp, ncent = lax.axis_size("dp"), lax.axis_size("cent")
    n, width = embeddings.shape
    own, k = centroids.shape
    chunks = 2
    w = n // (8 * chunks)
    groups = k // GROUP
    line = math.isqrt(ndp)
    dma = pltpu.SemaphoreType.DMA
    out = pl.pallas_call(
        functools.partial(kernel, ndp, ncent, chunks),
        out_shape=pltpu.VMEM((own, k), f32),
        in_specs=[pl.BlockSpec(memory_space=pl.ANY), pl.BlockSpec(memory_space=pl.ANY)],
        out_specs=pl.BlockSpec(memory_space=pltpu.VMEM),
        scratch_shapes=[
            pltpu.VMEM((n, width), bf16),
            pltpu.VMEM((own, k), bf16),
            pltpu.VMEM((width, k), bf16),
            pltpu.VMEM((k, width), bf16),
            pltpu.VMEM((k, n), f32),
            pltpu.VMEM((k, n), bf16),
            pltpu.VMEM((groups, width, GROUP), f32),
            pltpu.VMEM((groups, width, GROUP), bf16),
            pltpu.VMEM((ROUNDS, chunks, 8, w), f32),
            pltpu.VMEM((ROUNDS, chunks, ncent - 1, 8, w), f32),
            pltpu.VMEM((8, n), f32),
            pltpu.VMEM((8, n), f32),
            pltpu.VMEM((ROUNDS - 1, groups, LANES), f32),
            pltpu.VMEM((ROUNDS - 1, ndp - 1, groups, LANES), f32),
            pltpu.VMEM((groups, LANES), f32),
            pltpu.VMEM((ndp - 1, groups, LANES), f32),
            pltpu.VMEM((chunks, k, LANES), f32),
            pltpu.VMEM((chunks, k, LANES), f32),
            pltpu.VMEM((k, LANES), f32),
            pltpu.VMEM((groups, (line - 1) ** 2, own, GROUP), bf16),
            pltpu.VMEM((groups, 2 * (line - 1), own, GROUP), f32),
            pltpu.VMEM((groups, 2 * (line - 1), own, GROUP), f32),
            dma,
            dma((E_PARTS,)),
            dma((HALVES, 2 * (line - 1))),
            dma((HALVES,)),
            dma((HALVES,)),
            dma((ROUNDS, chunks)),
            dma((ROUNDS, chunks)),
            dma((ROUNDS - 1,)),
            dma((ROUNDS - 1,)),
            dma,
            dma,
            dma((groups,)),
            dma((groups,)),
            dma((groups,)),
            dma((groups,)),
        ],
        compiler_params=pltpu.CompilerParams(
            collective_id=0, has_side_effects=True, vmem_limit_bytes=50 * 2**20
        ),
        name="sinkhorn",
    )(embeddings, centroids)
    return out.T


def solution(mesh):
    return jax.shard_map(
        body,
        mesh=mesh,
        in_specs=(P("dp", None), P("cent", "dp")),
        out_specs=P("cent", "dp"),
        check_vma=False,
    )
```

```python
import functools
import math

import jax
import jax.numpy as jnp
from jax import lax
from jax.experimental import pallas as pl
from jax.experimental.pallas import tpu as pltpu
from jax.sharding import PartitionSpec as P

MESH = pl.DeviceIdType.MESH
f32 = jnp.float32
bf16 = jnp.bfloat16
LANES = 128
GROUP = 128
ROUNDS = 3
E_PARTS = 4
HALVES = 2


def nt_dot(a, b):
    return lax.dot_general(a, b, (((1,), (1,)), ((), ())), preferred_element_type=f32)


def nn_dot(a, b):
    return lax.dot_general(a, b, (((1,), (0,)), ((), ())), preferred_element_type=f32)


def lse2(parts):
    top = functools.reduce(jnp.maximum, parts)
    return top + jnp.log2(functools.reduce(jnp.add, [jnp.exp2(p - top) for p in parts]))


def lane_sums(a):
    return jnp.sum(a.T, axis=0, keepdims=True)


def to_rows(row):
    return jnp.broadcast_to(row, (LANES, GROUP)).T


def kernel(
    ndp, ncent, chunks,
    e_hbm, c_hbm, out_ref,
    e, ct_own, ct, c, b, plan, sums, low,
    row_own, row_in, acc8, pot,
    col_own, col_in, mass_own, mass_in,
    peak, fac, part, diag_in, line_out, line_in,
    c_sem, e_sem, near_recv, ct_send, ct_recv, row_send, row_recv, col_send, col_recv,
    mass_send, mass_recv, diag_send, diag_recv, line_send, line_recv,
):
    n, width = e.shape
    k = c.shape[0]
    own = width // ndp
    ny = math.isqrt(ndp)
    nz = ndp // ny
    w = n // (8 * chunks)
    groups = k // GROUP
    half = k // HALVES
    total_ratio = math.log2((n * ndp) / (k * ncent))

    pending = []

    me = lax.axis_index("dp")
    mec = lax.axis_index("cent")
    my_z, my_y = me // ny, me % ny

    def hops(d, size):
        return min(d, size - d)

    offsets = [(dz, dy) for dz in range(nz) for dy in range(ny)][1:]
    offsets.sort(key=lambda o: -hops(o[0], nz) - hops(o[1], ny))
    nx = ncent // 2
    cent_offsets = [(dx, core) for dx in range(nx) for core in range(2)][1:]
    cent_offsets.sort(key=lambda o: -hops(o[0], nx))

    def dp_peer(dz, dy):
        return ((my_z + dz) % nz) * ny + (my_y + dy) % ny

    def cent_peer(dx, core):
        return ((mec // 2 + dx) % nx) * 2 + (mec + core) % 2

    c_copy = pltpu.make_async_copy(c_hbm, ct_own, c_sem)
    c_copy.start()
    barrier = pltpu.get_barrier_semaphore()
    for dz, dy in offsets:
        pl.semaphore_signal(barrier, inc=1, device_id={"dp": dp_peer(dz, dy)}, device_id_type=MESH)
    for o in cent_offsets:
        pl.semaphore_signal(barrier, inc=1, device_id={"cent": cent_peer(*o)}, device_id_type=MESH)

    e_copies = []
    step = n // E_PARTS
    for i in range(E_PARTS):
        rows = pl.ds(i * step, step)
        e_copies.append(pltpu.make_async_copy(e_hbm.at[rows], e.at[rows], e_sem.at[i]))
        e_copies[-1].start()

    c_copy.wait()

    def feats_of(dp):
        return pl.ds(pl.multiple_of(dp * own, own), own)

    mine = feats_of(me)
    ct[mine, :] = ct_own[...]

    pl.semaphore_wait(barrier, len(offsets) + ncent - 1)

    def routes(dz, dy):
        a, b_ = hops(dz, nz), hops(dy, ny)
        if a == b_ and a > 1:
            return (0, half // 2), (half // 2, half)
        if a > b_ or (a == b_ and dz == dy):
            return (0, half), None
        return None, (0, half)

    def send_ct(h, src, rows, part_, off, sem):
        cols = pl.ds(h * half + part_[0], part_[1] - part_[0])
        pltpu.make_async_remote_copy(
            src_ref=ct_own.at[:, cols] if src is ct_own else src.at[rows, cols], dst_ref=ct.at[rows, cols],
            send_sem=ct_send.at[h], recv_sem=sem,
            device_id={"dp": dp_peer(*off)}, device_id_type=MESH,
        ).start()

    def wait_ct(sem, h, blocks):
        part_ = ct.at[pl.ds(0, own * blocks), pl.ds(h * half, half)]
        pltpu.make_async_copy(part_, part_, sem).wait()

    lines = [(d, 0) for d in range(1, nz)] + [(0, d) for d in range(1, ny)]
    far_first = sorted(lines, key=lambda o: -hops(o[0], nz) - hops(o[1], ny))
    for h in range(HALVES):
        for off in far_first:
            send_ct(h, ct_own, mine, (0, half), off, near_recv.at[h, lines.index(off)])
        pending.append(functools.partial(wait_ct, ct_send.at[h], h, ndp - 1))
    for h in range(HALVES):
        for dz, dy in far_first[::-1]:
            wait_ct(near_recv.at[h, lines.index((dz, dy))], h, 1)
            rows = feats_of(dp_peer(nz - dz, ny - dy))
            for d in range(1, ny if dy == 0 else nz):
                off, both = ((0, d), (dz, d)) if dy == 0 else ((d, 0), (d, dy))
                part_ = routes(*both)[0 if dy == 0 else 1]
                if part_:
                    send_ct(h, ct, rows, part_, off, ct_recv.at[h])

    unit = 4.0 / math.sqrt(width) / math.log(2.0)
    wide = 2 * w

    def send_rows(r, ch):
        for j, o in enumerate(cent_offsets):
            pltpu.make_async_remote_copy(
                src_ref=row_own.at[r, ch], dst_ref=row_in.at[r, ch, j],
                send_sem=row_send.at[r, ch], recv_sem=row_recv.at[r, ch],
                device_id={"cent": cent_peer(*o)}, device_id_type=MESH,
            ).start()
        pending.append(lambda: wait_rows(row_send, r, ch))

    def wait_rows(sem, r, ch):
        part_ = row_in.at[r, ch]
        pltpu.make_async_copy(part_, part_, sem.at[r, ch]).wait()

    for copy in e_copies:
        copy.wait()
    for ch in range(chunks):
        for h in range(HALVES):
            rows = pl.ds(h * half, half)
            if ch == 0:
                wait_ct(ct_recv.at[h], h, ndp - 1 - len(lines))
                c[rows, :] = ct[:, rows].T
            for i in range(0, 8, 2):
                at = (ch * 8 + i) * w
                toks = pl.ds(at, wide)
                x = nt_dot(c[rows, :], e[toks, :]) * unit
                b[rows, toks] = x
                top = jnp.max(x, axis=0, keepdims=True)
                tot = jnp.sum(jnp.exp2(x - top), axis=0, keepdims=True)
                lse = top + jnp.log2(tot)
                if h == 0:
                    acc8[0:1, toks] = lse
                else:
                    lse = lse2([lse, acc8[0:1, toks]])
                    row_own[0, ch, i : i + 1, :] = lse[:, :w]
                    row_own[0, ch, i + 1 : i + 2, :] = lse[:, w:]
        send_rows(0, ch)

    tiles = n // (chunks * LANES)

    def tile(ch, i):
        return pl.ds(pl.multiple_of((ch * tiles + i) * LANES, LANES), LANES)

    def over_tiles(f, init):
        return lax.fori_loop(0, tiles, f, init, unroll=tiles)

    def spread_rows(ch, dense):
        for i in range(8):
            pot[0:1, pl.ds((ch * 8 + i) * w, w)] = dense[i : i + 1, :]

    def send_cols(r):
        for o, (dz, dy) in enumerate(offsets):
            pltpu.make_async_remote_copy(
                src_ref=col_own.at[r], dst_ref=col_in.at[r, o],
                send_sem=col_send.at[r], recv_sem=col_recv.at[r],
                device_id={"dp": dp_peer(dz, dy)}, device_id_type=MESH,
            ).start()
        pending.append(lambda: wait_cols(col_send, r))

    def wait_cols(sem, r):
        part_ = col_in.at[r]
        pltpu.make_async_copy(part_, part_, sem.at[r]).wait()

    for ch in range(chunks):
        wait_rows(row_recv, 0, ch)
        spread_rows(ch, -lse2([row_own[0, ch]] + [row_in[0, ch, j] for j in range(ncent - 1)]))
        for g in range(groups):
            gs = pl.ds(g * GROUP, GROUP)

            def top_step(i, m):
                return jnp.maximum(m, b[gs, tile(ch, i)] + pot[0:1, tile(ch, i)])

            m = over_tiles(top_step, jnp.full((GROUP, LANES), -jnp.inf, f32))
            m = jnp.broadcast_to(jnp.max(m, axis=1, keepdims=True), (GROUP, LANES))
            peak[ch, gs, :] = m

            def exp_step(i, a):
                x = jnp.exp2((b[gs, tile(ch, i)] + pot[0:1, tile(ch, i)]) - m)
                b[gs, tile(ch, i)] = x
                return a + x

            a = over_tiles(exp_step, jnp.zeros((GROUP, LANES), f32))
            lse = m.T[0:1, :] + jnp.log2(lane_sums(a))
            if ch > 0:
                lse = lse2([lse, col_own[0, g : g + 1, :]])
            col_own[0, g : g + 1, :] = lse
    send_cols(0)
    wait_cols(col_recv, 0)
    lse = lse2([col_own[0]] + [col_in[0, j] for j in range(ndp - 1)])
    for g in range(groups):
        gs = pl.ds(g * GROUP, GROUP)
        shift = total_ratio - to_rows(lse[g : g + 1, :])
        for ch in range(chunks):
            fac[ch, gs, :] = jnp.exp2(peak[ch, gs, :] + shift)

    def send_row_sums(r):
        for ch in range(chunks):
            for g in range(groups):
                gs = pl.ds(g * GROUP, GROUP)
                f = fac[ch, gs, :]

                def step_(i, _):
                    x = jnp.sum((b[gs, tile(ch, i)] * f).reshape(GROUP // 8, 8, LANES), axis=0)
                    if g > 0:
                        x = x + acc8[:, tile(ch, i)]
                    acc8[:, tile(ch, i)] = x
                    return 0

                over_tiles(step_, 0)
            for i in range(8):
                s = jnp.sum(acc8[:, pl.ds((ch * 8 + i) * w, w)], axis=0, keepdims=True)
                row_own[r, ch, i : i + 1, :] = s
            send_rows(r, ch)

    def take_row_sums(r, ch):
        wait_rows(row_recv, r, ch)
        dense = row_own[r, ch]
        for j in range(ncent - 1):
            dense = dense + row_in[r, ch, j]
        spread_rows(ch, 1.0 / dense)

    send_row_sums(1)
    for ch in range(chunks):
        take_row_sums(1, ch)
        for g in range(groups):
            gs = pl.ds(g * GROUP, GROUP)

            def col_step(i, a):
                return a + b[gs, tile(ch, i)] * pot[0:1, tile(ch, i)]

            a = over_tiles(col_step, jnp.zeros((GROUP, LANES), f32)) * fac[ch, gs, :]
            if ch > 0:
                a = a + part[gs, :]
            if ch < chunks - 1:
                part[gs, :] = a
            else:
                col_own[1, g : g + 1, :] = lane_sums(a)
    send_cols(1)
    wait_cols(col_recv, 1)
    tot = col_own[1]
    for j in range(ndp - 1):
        tot = tot + col_in[1, j]
    tot = (2.0**total_ratio) / tot
    for g in range(groups):
        gs = pl.ds(g * GROUP, GROUP)
        scale = to_rows(tot[g : g + 1, :])
        for ch in range(chunks):
            fac[ch, gs, :] = fac[ch, gs, :] * scale

    def make_plan(ch, g):
        gs = pl.ds(g * GROUP, GROUP)
        f = fac[ch, gs, :]

        def plan_step(i, a):
            x = (b[gs, tile(ch, i)] * f) * pot[0:1, tile(ch, i)]
            plan[gs, tile(ch, i)] = x.astype(bf16)
            return a + x

        a = over_tiles(plan_step, jnp.zeros((GROUP, LANES), f32))
        if ch > 0:
            a = a + part[gs, :]
        if ch < chunks - 1:
            part[gs, :] = a
        else:
            mass_own[g : g + 1, :] = lane_sums(a)

    send_row_sums(2)
    for ch in range(chunks):
        take_row_sums(2, ch)
        for g in range(groups if ch < chunks - 1 else 1):
            make_plan(ch, g)

    def wait_all(buf, sem):
        pltpu.make_async_copy(buf, buf, sem).wait()

    diag = [o for o in offsets if o[0] and o[1]]

    def by_z(g, dz, dy):
        a, b_ = hops(dz, nz), hops(dy, ny)
        if a == b_:
            return dz == dy if a == 1 else g % 2 == 0
        return a < b_

    def send_sums(src, dst, sems, g, peer):
        pltpu.make_async_remote_copy(
            src_ref=src, dst_ref=dst, send_sem=sems[0].at[g], recv_sem=sems[1].at[g],
            device_id={"dp": peer}, device_id_type=MESH,
        ).start()

    def start_sums(g):
        for j, (dz, dy) in enumerate(diag):
            there = dp_peer(dz, 0) if by_z(g, dz, dy) else dp_peer(0, dy)
            send_sums(low.at[g, feats_of(dp_peer(dz, dy)), :], diag_in.at[g, j], (diag_send, diag_recv), g, there)
        pending.append(functools.partial(wait_all, diag_in.at[g], diag_send.at[g]))

    def pass_sums(g):
        wait_all(diag_in.at[g], diag_recv.at[g])
        for j, off in enumerate(far_first):
            peer = dp_peer(*off)
            tot = sums[g, feats_of(peer), :]
            for i, (dz, dy) in enumerate(diag):
                if off == ((0, dy) if by_z(g, dz, dy) else (dz, 0)):
                    tot = tot + diag_in[g, i].astype(f32)
            line_out[g, j] = tot
            send_sums(line_out.at[g, j], line_in.at[g, j], (line_send, line_recv), g, peer)

    for g in range(groups):
        if g + 1 < groups:
            make_plan(chunks - 1, g + 1)
        s = nn_dot(plan[pl.ds(g * GROUP, GROUP), :], e[...]).T
        sums[g] = s
        low[g] = s.astype(bf16)
        start_sums(g)
        if g == max(groups - 2, 0):
            for o, (dz, dy) in enumerate(offsets):
                pltpu.make_async_remote_copy(
                    src_ref=mass_own, dst_ref=mass_in.at[o], send_sem=mass_send, recv_sem=mass_recv,
                    device_id={"dp": dp_peer(dz, dy)}, device_id_type=MESH,
                ).start()
            pending.append(lambda: wait_all(mass_in, mass_send))
    for g in range(groups):
        pass_sums(g)

    for wait in pending:
        wait()

    wait_all(mass_in, mass_recv)
    mass = mass_own[...]
    for j in range(ndp - 1):
        mass = mass + mass_in[j]
    for g in range(groups):
        tot = sums[g, mine, :]
        wait_all(line_in.at[g], line_recv.at[g])
        for j in range(len(lines)):
            tot = tot + line_in[g, j]
        out_ref[:, pl.ds(g * GROUP, GROUP)] = tot / mass[g : g + 1, :]
    for g in range(groups):
        wait_all(line_in.at[g], line_send.at[g])


def body(embeddings, centroids):
    centroids = centroids.T
    embeddings = pltpu.with_memory_space_constraint(embeddings, pltpu.HBM)
    centroids = pltpu.with_memory_space_constraint(centroids, pltpu.HBM)
    ndp, ncent = lax.axis_size("dp"), lax.axis_size("cent")
    n, width = embeddings.shape
    own, k = centroids.shape
    chunks = 2
    w = n // (8 * chunks)
    groups = k // GROUP
    line = math.isqrt(ndp)
    dma = pltpu.SemaphoreType.DMA
    out = pl.pallas_call(
        functools.partial(kernel, ndp, ncent, chunks),
        out_shape=pltpu.VMEM((own, k), f32),
        in_specs=[pl.BlockSpec(memory_space=pl.ANY), pl.BlockSpec(memory_space=pl.ANY)],
        out_specs=pl.BlockSpec(memory_space=pltpu.VMEM),
        scratch_shapes=[
            pltpu.VMEM((n, width), bf16),
            pltpu.VMEM((own, k), bf16),
            pltpu.VMEM((width, k), bf16),
            pltpu.VMEM((k, width), bf16),
            pltpu.VMEM((k, n), f32),
            pltpu.VMEM((k, n), bf16),
            pltpu.VMEM((groups, width, GROUP), f32),
            pltpu.VMEM((groups, width, GROUP), bf16),
            pltpu.VMEM((ROUNDS, chunks, 8, w), f32),
            pltpu.VMEM((ROUNDS, chunks, ncent - 1, 8, w), f32),
            pltpu.VMEM((8, n), f32),
            pltpu.VMEM((8, n), f32),
            pltpu.VMEM((ROUNDS - 1, groups, LANES), f32),
            pltpu.VMEM((ROUNDS - 1, ndp - 1, groups, LANES), f32),
            pltpu.VMEM((groups, LANES), f32),
            pltpu.VMEM((ndp - 1, groups, LANES), f32),
            pltpu.VMEM((chunks, k, LANES), f32),
            pltpu.VMEM((chunks, k, LANES), f32),
            pltpu.VMEM((k, LANES), f32),
            pltpu.VMEM((groups, (line - 1) ** 2, own, GROUP), bf16),
            pltpu.VMEM((groups, 2 * (line - 1), own, GROUP), f32),
            pltpu.VMEM((groups, 2 * (line - 1), own, GROUP), f32),
            dma,
            dma((E_PARTS,)),
            dma((HALVES, 2 * (line - 1))),
            dma((HALVES,)),
            dma((HALVES,)),
            dma((ROUNDS, chunks)),
            dma((ROUNDS, chunks)),
            dma((ROUNDS - 1,)),
            dma((ROUNDS - 1,)),
            dma,
            dma,
            dma((groups,)),
            dma((groups,)),
            dma((groups,)),
            dma((groups,)),
        ],
        compiler_params=pltpu.CompilerParams(
            collective_id=0, has_side_effects=True, vmem_limit_bytes=50 * 2**20
        ),
        name="sinkhorn",
    )(embeddings, centroids)
    return out.T


def solution(mesh):
    return jax.shard_map(
        body,
        mesh=mesh,
        in_specs=(P("dp", None), P("cent", "dp")),
        out_specs=P("cent", "dp"),
        check_vma=False,
    )
```

```python
import functools
import math

import jax
import jax.numpy as jnp
from jax import lax
from jax.experimental import pallas as pl
from jax.experimental.pallas import tpu as pltpu
from jax.sharding import PartitionSpec as P

MESH = pl.DeviceIdType.MESH
f32 = jnp.float32
bf16 = jnp.bfloat16
LANES = 128
GROUP = 128
ROUNDS = 3
E_PARTS = 4
HALVES = 2


def nt_dot(a, b):
    return lax.dot_general(a, b, (((1,), (1,)), ((), ())), preferred_element_type=f32)


def nn_dot(a, b):
    return lax.dot_general(a, b, (((1,), (0,)), ((), ())), preferred_element_type=f32)


def lse2(parts):
    top = functools.reduce(jnp.maximum, parts)
    return top + jnp.log2(functools.reduce(jnp.add, [jnp.exp2(p - top) for p in parts]))


def lane_sums(a):
    return jnp.sum(a.T, axis=0, keepdims=True)


def to_rows(row):
    return jnp.broadcast_to(row, (LANES, GROUP)).T


def kernel(
    ndp, ncent, chunks,
    e_hbm, c_hbm, out_ref,
    e, ct_own, ct, c, b, plan, sums, low,
    row_own, row_in, acc8, pot,
    col_own, col_in, mass_own, mass_in,
    peak, fac, part, diag_in, line_out, line_in,
    c_sem, e_sem, near_recv, ct_send, ct_recv, row_send, row_recv, col_send, col_recv,
    mass_send, mass_recv, diag_send, diag_recv, line_send, line_recv,
):
    n, width = e.shape
    k = c.shape[0]
    own = width // ndp
    ny = math.isqrt(ndp)
    nz = ndp // ny
    w = n // (8 * chunks)
    groups = k // GROUP
    half = k // HALVES
    total_ratio = math.log2((n * ndp) / (k * ncent))

    pending = []

    me = lax.axis_index("dp")
    mec = lax.axis_index("cent")
    my_z, my_y = me // ny, me % ny

    def hops(d, size):
        return min(d, size - d)

    offsets = [(dz, dy) for dz in range(nz) for dy in range(ny)][1:]
    offsets.sort(key=lambda o: -hops(o[0], nz) - hops(o[1], ny))
    nx = ncent // 2
    cent_offsets = [(dx, core) for dx in range(nx) for core in range(2)][1:]
    cent_offsets.sort(key=lambda o: -hops(o[0], nx))

    def dp_peer(dz, dy):
        return ((my_z + dz) % nz) * ny + (my_y + dy) % ny

    def cent_peer(dx, core):
        return ((mec // 2 + dx) % nx) * 2 + (mec + core) % 2

    c_copy = pltpu.make_async_copy(c_hbm, ct_own, c_sem)
    c_copy.start()
    barrier = pltpu.get_barrier_semaphore()
    for dz, dy in offsets:
        pl.semaphore_signal(barrier, inc=1, device_id={"dp": dp_peer(dz, dy)}, device_id_type=MESH)
    for o in cent_offsets:
        pl.semaphore_signal(barrier, inc=1, device_id={"cent": cent_peer(*o)}, device_id_type=MESH)

    e_copies = []
    step = n // E_PARTS
    for i in range(E_PARTS):
        rows = pl.ds(i * step, step)
        e_copies.append(pltpu.make_async_copy(e_hbm.at[rows], e.at[rows], e_sem.at[i]))
        e_copies[-1].start()

    c_copy.wait()

    def feats_of(dp):
        return pl.ds(pl.multiple_of(dp * own, own), own)

    mine = feats_of(me)
    ct[mine, :] = ct_own[...]

    pl.semaphore_wait(barrier, len(offsets) + ncent - 1)

    def routes(dz, dy):
        a, b_ = hops(dz, nz), hops(dy, ny)
        if a == b_ and a > 1:
            return (0, half // 2), (half // 2, half)
        if a > b_ or (a == b_ and dz == dy):
            return (0, half), None
        return None, (0, half)

    def send_ct(h, src, rows, part_, off, sem):
        cols = pl.ds(h * half + part_[0], part_[1] - part_[0])
        pltpu.make_async_remote_copy(
            src_ref=ct_own.at[:, cols] if src is ct_own else src.at[rows, cols], dst_ref=ct.at[rows, cols],
            send_sem=ct_send.at[h], recv_sem=sem,
            device_id={"dp": dp_peer(*off)}, device_id_type=MESH,
        ).start()

    def wait_ct(sem, h, blocks):
        part_ = ct.at[pl.ds(0, own * blocks), pl.ds(h * half, half)]
        pltpu.make_async_copy(part_, part_, sem).wait()

    lines = [(d, 0) for d in range(1, nz)] + [(0, d) for d in range(1, ny)]
    far_first = sorted(lines, key=lambda o: -hops(o[0], nz) - hops(o[1], ny))
    for h in range(HALVES):
        for off in far_first:
            send_ct(h, ct_own, mine, (0, half), off, near_recv.at[h, lines.index(off)])
        pending.append(functools.partial(wait_ct, ct_send.at[h], h, ndp - 1))
    for h in range(HALVES):
        for dz, dy in far_first[::-1]:
            wait_ct(near_recv.at[h, lines.index((dz, dy))], h, 1)
            rows = feats_of(dp_peer(nz - dz, ny - dy))
            for d in range(1, ny if dy == 0 else nz):
                off, both = ((0, d), (dz, d)) if dy == 0 else ((d, 0), (d, dy))
                part_ = routes(*both)[0 if dy == 0 else 1]
                if part_:
                    send_ct(h, ct, rows, part_, off, ct_recv.at[h])

    unit = 4.0 / math.sqrt(width) / math.log(2.0)
    wide = 2 * w

    def send_rows(r, ch):
        for j, o in enumerate(cent_offsets):
            pltpu.make_async_remote_copy(
                src_ref=row_own.at[r, ch], dst_ref=row_in.at[r, ch, j],
                send_sem=row_send.at[r, ch], recv_sem=row_recv.at[r, ch],
                device_id={"cent": cent_peer(*o)}, device_id_type=MESH,
            ).start()
        pending.append(lambda: wait_rows(row_send, r, ch))

    def wait_rows(sem, r, ch):
        part_ = row_in.at[r, ch]
        pltpu.make_async_copy(part_, part_, sem.at[r, ch]).wait()

    for copy in e_copies:
        copy.wait()
    for ch in range(chunks):
        for h in range(HALVES):
            rows = pl.ds(h * half, half)
            if ch == 0:
                wait_ct(ct_recv.at[h], h, ndp - 1 - len(lines))
                c[rows, :] = ct[:, rows].T
            for i in range(0, 8, 2):
                at = (ch * 8 + i) * w
                toks = pl.ds(at, wide)
                x = nt_dot(c[rows, :], e[toks, :]) * unit
                b[rows, toks] = x
                top = jnp.max(x, axis=0, keepdims=True)
                tot = jnp.sum(jnp.exp2(x - top), axis=0, keepdims=True)
                lse = top + jnp.log2(tot)
                if h == 0:
                    acc8[0:1, toks] = lse
                else:
                    lse = lse2([lse, acc8[0:1, toks]])
                    row_own[0, ch, i : i + 1, :] = lse[:, :w]
                    row_own[0, ch, i + 1 : i + 2, :] = lse[:, w:]
        send_rows(0, ch)

    tiles = n // (chunks * LANES)

    def tile(ch, i):
        return pl.ds(pl.multiple_of((ch * tiles + i) * LANES, LANES), LANES)

    def over_tiles(f, init):
        return lax.fori_loop(0, tiles, f, init, unroll=tiles)

    def spread_rows(ch, dense):
        for i in range(8):
            pot[0:1, pl.ds((ch * 8 + i) * w, w)] = dense[i : i + 1, :]

    def send_cols(r):
        for o, (dz, dy) in enumerate(offsets):
            pltpu.make_async_remote_copy(
                src_ref=col_own.at[r], dst_ref=col_in.at[r, o],
                send_sem=col_send.at[r], recv_sem=col_recv.at[r],
                device_id={"dp": dp_peer(dz, dy)}, device_id_type=MESH,
            ).start()
        pending.append(lambda: wait_cols(col_send, r))

    def wait_cols(sem, r):
        part_ = col_in.at[r]
        pltpu.make_async_copy(part_, part_, sem.at[r]).wait()

    for ch in range(chunks):
        wait_rows(row_recv, 0, ch)
        spread_rows(ch, -lse2([row_own[0, ch]] + [row_in[0, ch, j] for j in range(ncent - 1)]))
        for g in range(groups):
            gs = pl.ds(g * GROUP, GROUP)

            def top_step(i, m):
                return jnp.maximum(m, b[gs, tile(ch, i)] + pot[0:1, tile(ch, i)])

            m = over_tiles(top_step, jnp.full((GROUP, LANES), -jnp.inf, f32))
            m = jnp.broadcast_to(jnp.max(m, axis=1, keepdims=True), (GROUP, LANES))
            peak[ch, gs, :] = m

            def exp_step(i, a):
                x = jnp.exp2((b[gs, tile(ch, i)] + pot[0:1, tile(ch, i)]) - m)
                b[gs, tile(ch, i)] = x
                return a + x

            a = over_tiles(exp_step, jnp.zeros((GROUP, LANES), f32))
            lse = m.T[0:1, :] + jnp.log2(lane_sums(a))
            if ch > 0:
                lse = lse2([lse, col_own[0, g : g + 1, :]])
            col_own[0, g : g + 1, :] = lse
    send_cols(0)
    wait_cols(col_recv, 0)
    lse = lse2([col_own[0]] + [col_in[0, j] for j in range(ndp - 1)])
    for g in range(groups):
        gs = pl.ds(g * GROUP, GROUP)
        shift = total_ratio - to_rows(lse[g : g + 1, :])
        for ch in range(chunks):
            fac[ch, gs, :] = jnp.exp2(peak[ch, gs, :] + shift)

    def send_row_sums(r):
        for ch in range(chunks):
            for g in range(groups):
                gs = pl.ds(g * GROUP, GROUP)
                f = fac[ch, gs, :]

                def step_(i, _):
                    x = jnp.sum((b[gs, tile(ch, i)] * f).reshape(GROUP // 8, 8, LANES), axis=0)
                    if g > 0:
                        x = x + acc8[:, tile(ch, i)]
                    acc8[:, tile(ch, i)] = x
                    return 0

                over_tiles(step_, 0)
            for i in range(8):
                s = jnp.sum(acc8[:, pl.ds((ch * 8 + i) * w, w)], axis=0, keepdims=True)
                row_own[r, ch, i : i + 1, :] = s
            send_rows(r, ch)

    def take_row_sums(r, ch):
        wait_rows(row_recv, r, ch)
        dense = row_own[r, ch]
        for j in range(ncent - 1):
            dense = dense + row_in[r, ch, j]
        spread_rows(ch, 1.0 / dense)

    send_row_sums(1)
    for ch in range(chunks):
        take_row_sums(1, ch)
        for g in range(groups):
            gs = pl.ds(g * GROUP, GROUP)

            def col_step(i, a):
                return a + b[gs, tile(ch, i)] * pot[0:1, tile(ch, i)]

            a = over_tiles(col_step, jnp.zeros((GROUP, LANES), f32)) * fac[ch, gs, :]
            if ch > 0:
                a = a + part[gs, :]
            if ch < chunks - 1:
                part[gs, :] = a
            else:
                col_own[1, g : g + 1, :] = lane_sums(a)
    send_cols(1)
    wait_cols(col_recv, 1)
    tot = col_own[1]
    for j in range(ndp - 1):
        tot = tot + col_in[1, j]
    tot = (2.0**total_ratio) / tot
    for g in range(groups):
        gs = pl.ds(g * GROUP, GROUP)
        scale = to_rows(tot[g : g + 1, :])
        for ch in range(chunks):
            fac[ch, gs, :] = fac[ch, gs, :] * scale

    def make_plan(ch, g):
        gs = pl.ds(g * GROUP, GROUP)
        f = fac[ch, gs, :]

        def plan_step(i, a):
            x = (b[gs, tile(ch, i)] * f) * pot[0:1, tile(ch, i)]
            plan[gs, tile(ch, i)] = x.astype(bf16)
            return a + x

        a = over_tiles(plan_step, jnp.zeros((GROUP, LANES), f32))
        if ch > 0:
            a = a + part[gs, :]
        if ch < chunks - 1:
            part[gs, :] = a
        else:
            mass_own[g : g + 1, :] = lane_sums(a)

    send_row_sums(2)
    for ch in range(chunks):
        take_row_sums(2, ch)
        for g in range(groups if ch < chunks - 1 else 1):
            make_plan(ch, g)

    def wait_all(buf, sem):
        pltpu.make_async_copy(buf, buf, sem).wait()

    diag = [o for o in offsets if o[0] and o[1]]

    def by_z(g, dz, dy):
        a, b_ = hops(dz, nz), hops(dy, ny)
        if a == b_:
            return dz == dy if a == 1 else g % 2 == 0
        return a < b_

    def send_sums(src, dst, sems, g, peer):
        pltpu.make_async_remote_copy(
            src_ref=src, dst_ref=dst, send_sem=sems[0].at[g], recv_sem=sems[1].at[g],
            device_id={"dp": peer}, device_id_type=MESH,
        ).start()

    def start_sums(g):
        for j, (dz, dy) in enumerate(diag):
            there = dp_peer(dz, 0) if by_z(g, dz, dy) else dp_peer(0, dy)
            send_sums(low.at[g, feats_of(dp_peer(dz, dy)), :], diag_in.at[g, j], (diag_send, diag_recv), g, there)
        pending.append(functools.partial(wait_all, diag_in.at[g], diag_send.at[g]))

    def pass_sums(g):
        wait_all(diag_in.at[g], diag_recv.at[g])
        for j, off in enumerate(far_first):
            peer = dp_peer(*off)
            tot = sums[g, feats_of(peer), :]
            for i, (dz, dy) in enumerate(diag):
                if off == ((0, dy) if by_z(g, dz, dy) else (dz, 0)):
                    tot = tot + diag_in[g, i].astype(f32)
            line_out[g, j] = tot
            send_sums(line_out.at[g, j], line_in.at[g, j], (line_send, line_recv), g, peer)

    for g in range(groups):
        if g + 1 < groups:
            make_plan(chunks - 1, g + 1)
        s = nn_dot(plan[pl.ds(g * GROUP, GROUP), :], e[...]).T
        sums[g] = s
        low[g] = s.astype(bf16)
        start_sums(g)
    for o, (dz, dy) in enumerate(offsets):
        pltpu.make_async_remote_copy(
            src_ref=mass_own, dst_ref=mass_in.at[o], send_sem=mass_send, recv_sem=mass_recv,
            device_id={"dp": dp_peer(dz, dy)}, device_id_type=MESH,
        ).start()
    pending.append(lambda: wait_all(mass_in, mass_send))
    for g in range(groups):
        pass_sums(g)

    for wait in pending:
        wait()

    wait_all(mass_in, mass_recv)
    mass = mass_own[...]
    for j in range(ndp - 1):
        mass = mass + mass_in[j]
    for g in range(groups):
        tot = sums[g, mine, :]
        wait_all(line_in.at[g], line_recv.at[g])
        for j in range(len(lines)):
            tot = tot + line_in[g, j]
        out_ref[:, pl.ds(g * GROUP, GROUP)] = tot / mass[g : g + 1, :]
    for g in range(groups):
        wait_all(line_in.at[g], line_send.at[g])


def body(embeddings, centroids):
    centroids = centroids.T
    embeddings = pltpu.with_memory_space_constraint(embeddings, pltpu.HBM)
    centroids = pltpu.with_memory_space_constraint(centroids, pltpu.HBM)
    ndp, ncent = lax.axis_size("dp"), lax.axis_size("cent")
    n, width = embeddings.shape
    own, k = centroids.shape
    chunks = 2
    w = n // (8 * chunks)
    groups = k // GROUP
    line = math.isqrt(ndp)
    dma = pltpu.SemaphoreType.DMA
    out = pl.pallas_call(
        functools.partial(kernel, ndp, ncent, chunks),
        out_shape=pltpu.VMEM((own, k), f32),
        in_specs=[pl.BlockSpec(memory_space=pl.ANY), pl.BlockSpec(memory_space=pl.ANY)],
        out_specs=pl.BlockSpec(memory_space=pltpu.VMEM),
        scratch_shapes=[
            pltpu.VMEM((n, width), bf16),
            pltpu.VMEM((own, k), bf16),
            pltpu.VMEM((width, k), bf16),
            pltpu.VMEM((k, width), bf16),
            pltpu.VMEM((k, n), f32),
            pltpu.VMEM((k, n), bf16),
            pltpu.VMEM((groups, width, GROUP), f32),
            pltpu.VMEM((groups, width, GROUP), bf16),
            pltpu.VMEM((ROUNDS, chunks, 8, w), f32),
            pltpu.VMEM((ROUNDS, chunks, ncent - 1, 8, w), f32),
            pltpu.VMEM((8, n), f32),
            pltpu.VMEM((8, n), f32),
            pltpu.VMEM((ROUNDS - 1, groups, LANES), f32),
            pltpu.VMEM((ROUNDS - 1, ndp - 1, groups, LANES), f32),
            pltpu.VMEM((groups, LANES), f32),
            pltpu.VMEM((ndp - 1, groups, LANES), f32),
            pltpu.VMEM((chunks, k, LANES), f32),
            pltpu.VMEM((chunks, k, LANES), f32),
            pltpu.VMEM((k, LANES), f32),
            pltpu.VMEM((groups, (line - 1) ** 2, own, GROUP), bf16),
            pltpu.VMEM((groups, 2 * (line - 1), own, GROUP), f32),
            pltpu.VMEM((groups, 2 * (line - 1), own, GROUP), f32),
            dma,
            dma((E_PARTS,)),
            dma((HALVES, 2 * (line - 1))),
            dma((HALVES,)),
            dma((HALVES,)),
            dma((ROUNDS, chunks)),
            dma((ROUNDS, chunks)),
            dma((ROUNDS - 1,)),
            dma((ROUNDS - 1,)),
            dma,
            dma,
            dma((groups,)),
            dma((groups,)),
            dma((groups,)),
            dma((groups,)),
        ],
        compiler_params=pltpu.CompilerParams(
            collective_id=0, has_side_effects=True, vmem_limit_bytes=50 * 2**20
        ),
        name="sinkhorn",
    )(embeddings, centroids)
    return out.T


def solution(mesh):
    return jax.shard_map(
        body,
        mesh=mesh,
        in_specs=(P("dp", None), P("cent", "dp")),
        out_specs=P("cent", "dp"),
        check_vma=False,
    )
```
